32 devices in a mesh: ctx: 4 (over y, x), exp: 8 (over z, core).
Axes of the slice: x: 2, y: 2, z: 4, core: 2. Of those that a mesh axis runs over, the one named last changes fastest.
Arguments:
- query_heads: bfloat16 [1024, 8, 128], P('ctx', 'exp'), may hold values from -0.59765625 to 0.59765625
- key_heads: bfloat16 [1024, 8, 128], P('ctx', 'exp'), may hold values from -0.59765625 to 0.59765625
- value_heads: bfloat16 [1024, 8, 128], P('ctx', 'exp'), may hold values from -6 to 6
- out_grad: bfloat16 [1024, 8, 128], P('ctx', 'exp'), may hold values from -0.29882812 to 0.29882812
- log_decay: bfloat16 [1024, 8, 128], P('ctx', 'exp'), may hold values from -1 to 0, as said below
- start_state: float32 [4, 8, 128, 128], P('ctx', 'exp'), may hold values from -24 to 24
- layer_grad: bfloat16 [1024, 2304], P(('ctx', 'exp')), may hold values from -6 to 6
- gate_weights: float32 [1024, 8], P(('ctx', 'exp')), may hold values from 0.1 to 1
- routes: int32 [1024, 8], P(('ctx', 'exp')), may hold values from 0 to 31, all different within a row; in each aligned block of 32 rows (0 to 31, 32 to 63, ...) at most 16 rows name the same one
- expert_down: bfloat16 [32, 512, 2304], P('exp'), may hold values from -0.125 to 0.125
Outputs:
- query_grad: bfloat16 [1024, 8, 128], P('ctx', 'exp')
- key_grad: bfloat16 [1024, 8, 128], P('ctx', 'exp')
- value_grad: bfloat16 [1024, 8, 128], P('ctx', 'exp')
- hidden_grad: bfloat16 [4, 8, 32, 16, 512], P('ctx', None, 'exp')
The draws below stay inside these ranges and needn't reach their ends.
Inputs may be any that keep to these rules, and one draw needn't show every extreme that they name: `routes`: each row names 8 different experts. Within the 32 rows of one device no expert is named by more than 16 rows, a bound that some block reaches. `log_decay`: every entry is at most zero.
All inputs are finite; a program needn't handle non-finite values.
Results may differ from the reference program's by a relative error of at most 0.0049.
Values may be sent and summed in bfloat16 or wider, within the bound.
A program may use at most 64 MiB of HBM per device.

```python
import math
import jax
import jax.numpy as jnp
import numpy as np
from jax import lax

D = 2304
KD = 128
VD = 128
TOP = 8
FW = 512
EXPERTS = 32
ROWS_DEV = 32
HEADS = 8
MOST = 16
TOK_CTX = 256
STREAM_POSITIONS = 1024
GROUPS = 4
SOURCES = 8


def draw_log_decay(key, part):
    key = jax.random.fold_in(key, 11)
    addressing_array = jax.random.split(key, 10)
    slow_share = 0.5
    chooser = jax.random.uniform(addressing_array[0], (HEADS, KD))
    slow_rate = jnp.exp(jax.random.uniform(addressing_array[1], (HEADS, KD), minval=math.log(0.05), maxval=math.log(0.5))) / STREAM_POSITIONS
    fast_rate = jnp.exp(jax.random.uniform(addressing_array[2], (HEADS, KD), minval=math.log(1.0 / 50.0), maxval=math.log(1.0 / 25.0)))
    arriving_rate_count = jnp.where(chooser < slow_share, slow_rate, fast_rate)
    segments = (STREAM_POSITIONS + 63) // 64
    segment_factor = jnp.exp(jax.random.uniform(addressing_array[3], (segments, HEADS, 1), minval=-0.7, maxval=0.7))
    forgetting_multiplier = jnp.repeat(segment_factor, 64, axis=0)[:STREAM_POSITIONS]
    per_position_forgetting = jnp.exp(jax.random.uniform(addressing_array[4], (STREAM_POSITIONS, HEADS, KD), minval=-0.35, maxval=0.35))
    cluster_delivered = jax.random.bernoulli(addressing_array[5], 3.0 / STREAM_POSITIONS, (STREAM_POSITIONS, 1, 1))
    cluster_extent = jax.random.uniform(addressing_array[6], (STREAM_POSITIONS, 1, 1), minval=math.log(0.5), maxval=math.log(0.8))
    content_array = -arriving_rate_count[None, :, :] * forgetting_multiplier * per_position_forgetting + jnp.where(cluster_delivered, cluster_extent, 0.0)
    stretch_length = min(384, STREAM_POSITIONS // 4)
    stretch_start = jax.random.randint(addressing_array[7], (1, HEADS, 1), 0, STREAM_POSITIONS - stretch_length + 1)
    positions = jnp.arange(STREAM_POSITIONS, dtype=jnp.int32)[:, None, None]
    within_stretch = (positions >= stretch_start) & (positions < stretch_start + stretch_length)
    stretch_channel = jax.random.uniform(addressing_array[8], (1, HEADS, KD)) < 0.0625
    steep_values = jax.random.uniform(addressing_array[9], (STREAM_POSITIONS, HEADS, KD), minval=-1.0, maxval=-0.6)
    content_array = jnp.where(within_stretch & stretch_channel, steep_values, content_array)
    return content_array.astype(jnp.float32).astype(jnp.bfloat16)


def block_levels(stream_key, extent, pieces, least, high):
    def one(dim, blocks):
        steps = jax.random.uniform(jax.random.fold_in(jax.random.fold_in(stream_key, 6), dim), (blocks,), jnp.float32, least / len(pieces), high / len(pieces))
        return jnp.repeat(jnp.exp(steps), extent[dim] // blocks).reshape((-1,) + (1,) * (len(extent) - dim - 1))

    level = one(*pieces[0])
    for cut in pieces[1:]:
        level = level * one(*cut)
    return level


def shared_out(rng, own, number, rows, amount, top, most, slope):
    sequence = jax.random.permutation(rng, amount)
    packed, usual = portions_of(amount, rows * top, most, slope, True), portions_of(amount, rows * top, most, slope, False)
    places = jnp.arange(amount)

    def named(lengths, turn):
        used = int((lengths > 0).sum())
        fixed = max(1, used // 4)
        moved = fixed + (places - fixed + turn * (used - fixed)) % max(1, amount - fixed)
        return jnp.zeros((amount,), jnp.int32).at[sequence[jnp.where(places < fixed, places, moved)]].set(jnp.asarray(lengths, jnp.int32))

    lengths = jnp.where(number % 4 == 0, named(packed, number // 4), named(usual, number - number // 4 - 1))
    mixed = jax.random.permutation(jax.random.fold_in(own, 3), amount)
    giver, taker = mixed[0:amount // 2 * 2:2], mixed[1:amount // 2 * 2:2]
    margin = jnp.minimum(lengths[giver] - 1, most - lengths[taker]) // 2
    margin = jnp.where((giver == sequence[0]) | (taker == sequence[0]) | (lengths[taker] == 0), 0, jnp.maximum(margin, 0))
    moved = jax.random.randint(jax.random.fold_in(own, 4), (amount // 2,), 0, 1 << 20) % (margin + 1)
    lengths = lengths.at[giver].add(-moved).at[taker].add(moved)
    items = jnp.searchsorted(jnp.cumsum(lengths), jnp.arange(rows * top), side="right").astype(jnp.int32)
    table = items.reshape(top, rows).T
    table = table[jax.random.permutation(jax.random.fold_in(own, 1), rows)]
    turn = jax.random.randint(jax.random.fold_in(own, 2), (rows, 1), 0, top)
    return jnp.take_along_axis(table, (jnp.arange(top)[None, :] + turn) % top, axis=1)


def portions_of(number_of, total, limit, slope, full):
    weights = [(1 << 20) // math.isqrt(grade ** slope) + 1 for grade in range(1, number_of + 1)]
    largest = limit if full else min(limit, max(-(-total // number_of), total * weights[0] // sum(weights)))
    least = 1 if total - largest >= number_of - 1 else 0
    holding, rest = [largest] + [least] * (number_of - 1), total - largest - least * (number_of - 1)
    while rest > 0:
        candidates = [i for i in range(1, number_of) if holding[i] < largest] or [i for i in range(1, number_of) if holding[i] < limit]
        mass, left = sum([weights[i] for i in candidates]), rest
        for i in candidates:
            extra = min(limit - holding[i], max(1, left * weights[i] // mass), rest)
            holding[i] = holding[i] + extra
            rest = rest - extra
    return np.array(holding)


def gaussian(key, dims, scale, most, pieces=(), kind=jnp.bfloat16):
    result = jax.random.normal(key, dims, jnp.float32) * scale
    if len(pieces) > 0:
        result = block_levels(key, dims, pieces, -0.22, 0.18) * result
    return jnp.clip(result, min=-most, max=most).astype(kind)


def setup_inputs(seed: int = 0) -> dict:
    key_of = jax.random.split(jax.random.key(seed), 11)
    query_heads = gaussian(key_of[0], (STREAM_POSITIONS, HEADS, KD), 0.088, 0.59765625, ((0, 4), (1, 8)))
    key_heads = gaussian(key_of[1], (STREAM_POSITIONS, HEADS, KD), 0.088, 0.59765625, ((0, 4), (1, 8)))
    value_heads = gaussian(key_of[2], (STREAM_POSITIONS, HEADS, VD), 1.0, 6.0, ((0, 4), (1, 8)))
    out_grad = gaussian(key_of[3], (STREAM_POSITIONS, HEADS, VD), 0.05, 0.29882812, ((0, 4), (1, 8)))
    log_decay = draw_log_decay(jax.random.fold_in(key_of[10], 71), 0)
    start_state = gaussian(key_of[5], (GROUPS, HEADS, KD, VD), 4.0, 24.0, ((0, 4), (1, 8)), jnp.float32)
    layer_grad = gaussian(key_of[6], (STREAM_POSITIONS, D), 1.0, 6.0, ((0, 32),))
    gate_weights = jnp.clip(0.1 + 0.9 * jax.random.uniform(key_of[7], (STREAM_POSITIONS, TOP), jnp.float32) ** block_levels(key_of[7], (STREAM_POSITIONS, TOP), ((0, 32),), -0.2, 0.2), 0.1, 1.0)
    routes_keys = jax.random.split(jax.random.fold_in(key_of[8], 1), STREAM_POSITIONS // ROWS_DEV)
    routes_turns = jax.random.permutation(jax.random.fold_in(key_of[8], 3), STREAM_POSITIONS // ROWS_DEV)
    routes = jax.vmap(lambda own, number: shared_out(jax.random.fold_in(key_of[8], 2), own, number, ROWS_DEV, EXPERTS, TOP, MOST, 2))(routes_keys, routes_turns).reshape((STREAM_POSITIONS, TOP))
    expert_down = gaussian(key_of[9], (EXPERTS, FW, D), D ** -0.5, 0.125, ((0, 8),))
    return {"query_heads": query_heads, "key_heads": key_heads, "value_heads": value_heads, "out_grad": out_grad, "log_decay": log_decay, "start_state": start_state, "layer_grad": layer_grad, "gate_weights": gate_weights, "routes": routes, "expert_down": expert_down}


BEST_MATMUL_MODE = lax.Precision.HIGHEST


def group_forward(items):
    queries, key_rows, value_row_list, gradient_rows, decays, initial = items

    def advance(running_state, item):
        query_t, key_step, value_step, gradient_step, decay_t = item
        running_state = jnp.exp(decay_t)[:, :, None] * running_state + key_step[:, :, None] * value_step[:, None, :]
        return running_state, jnp.einsum("oig,og->oi", running_state, gradient_step, precision=BEST_MATMUL_MODE)

    return lax.scan(advance, initial, (queries, key_rows, value_row_list, gradient_rows, decays))[1]


def retreat(adjoint_state, item):
    query_t, key_step, value_step, gradient_step, decay_t = item
    adjoint_state = adjoint_state + query_t[:, :, None] * gradient_step[:, None, :]
    key_portion = jnp.einsum("oig,og->oi", adjoint_state, value_step, precision=BEST_MATMUL_MODE)
    value_portion = jnp.einsum("yau,ya->yu", adjoint_state, key_step, precision=BEST_MATMUL_MODE)
    return jnp.exp(decay_t)[:, :, None] * adjoint_state, (key_portion, value_portion)


def by_group(array):
    return array.reshape((GROUPS, TOK_CTX) + array.shape[1:])


def slot_positions(block_routes):
    flat = block_routes.reshape(-1)
    indicator_matrix = (flat[:, None] == jnp.arange(EXPERTS, dtype=jnp.int32)[None, :]).astype(jnp.int32)
    before = jnp.cumsum(indicator_matrix, axis=0) - indicator_matrix
    return flat * MOST + jnp.sum(before * indicator_matrix, axis=1)


def reference(query_heads, key_heads, value_heads, out_grad, log_decay, start_state, layer_grad, gate_weights, routes, expert_down):
    queries = query_heads.astype(jnp.float32)
    key_rows = key_heads.astype(jnp.float32)
    value_row_list = value_heads.astype(jnp.float32)
    gradient_rows = out_grad.astype(jnp.float32)
    decays = log_decay.astype(jnp.float32)
    grouped = (by_group(queries), by_group(key_rows), by_group(value_row_list), by_group(gradient_rows), by_group(decays), start_state)
    query_grad = lax.map(group_forward, grouped).reshape(queries.shape)
    initial = jnp.zeros((HEADS, KD, VD), jnp.float32)
    unused, parts = lax.scan(retreat, initial, (queries, key_rows, value_row_list, gradient_rows, decays), reverse=True)
    key_grad, value_grad = parts

    down_wide = expert_down.astype(jnp.float32)
    row_blocks = layer_grad.reshape(GROUPS * SOURCES, ROWS_DEV, D)
    gate_blocks = gate_weights.reshape(GROUPS * SOURCES, ROWS_DEV, TOP)
    route_blocks = routes.reshape(GROUPS * SOURCES, ROWS_DEV, TOP)

    def expert_block(items):
        grad_block, gate_block, route_block = items
        scaled = (gate_block[:, :, None] * grad_block[:, None, :].astype(jnp.float32)).astype(jnp.bfloat16).reshape(ROWS_DEV * TOP, D)
        position = slot_positions(route_block)
        buffer = jnp.zeros((EXPERTS * MOST, D), jnp.bfloat16).at[position].set(scaled).reshape(EXPERTS, MOST, D)
        product = jnp.einsum("emd,efd->emf", buffer.astype(jnp.float32), down_wide, precision=BEST_MATMUL_MODE)
        return product.astype(jnp.bfloat16)

    hidden_grad = lax.map(expert_block, (row_blocks, gate_blocks, route_blocks)).reshape(GROUPS, SOURCES, EXPERTS, MOST, FW)
    return (query_grad.astype(jnp.bfloat16), key_grad.astype(jnp.bfloat16), value_grad.astype(jnp.bfloat16), hidden_grad)
```

```python
import functools

import jax
import jax.numpy as jnp
from jax import lax
from jax.experimental import pallas as pl
from jax.experimental.pallas import tpu as pltpu
from jax.sharding import PartitionSpec as P

MOST = 16
F32 = jnp.float32
BF16 = jnp.bfloat16
MESH = pl.DeviceIdType.MESH


def dot(a, b, ca, cb):
    return lax.dot_general(a, b, (((ca,), (cb,)), ((), ())), preferred_element_type=F32)


def split(x):
    high = x.astype(BF16)
    return [high, (x - high.astype(F32)).astype(BF16)]


def mm(a, b, ca, cb):
    total = None
    for i, left in enumerate(a):
        for j, right in enumerate(b):
            if i + j < 2:
                term = dot(left, right, ca, cb)
                total = term if total is None else total + term
    return total


def kernel(
    groups, peers, chunk,
    q_hbm, k_hbm, v_hbm, g_hbm, d_hbm, s_hbm, x_hbm, gate_hbm, route_hbm, w_hbm,
    qg_hbm, kg_hbm, vg_hbm, out_hbm,
    q_ref, k_ref, v_ref, g_ref, d_ref, s_ref, gate_ref, route_ref, meta, xall, w_ref,
    pick, scale, slots, out_ref, qg_ref, kg_ref, vg_ref, message, arrived, carry, ed_ref, red_ref,
    kpart, vpart, mstate, lsem, wsem, osem, msend, mrecv, xown, xlocal, xsend, xrecv, csend, crecv,
):
    c = lax.axis_index("ctx")
    s = lax.axis_index("exp")
    z = s // 2
    h = s % 2
    line = peers // 2
    sibling = z * 2 + 1 - h
    length = q_ref.shape[0]
    count = length // chunk
    experts = w_ref.shape[0]
    tokens = xall.shape[1]

    barrier = pltpu.get_barrier_semaphore()
    for off in range(1, peers):
        pl.semaphore_signal(barrier, inc=1, device_id={"exp": (s + off) % peers}, device_id_type=MESH)
    for off in range(1, groups):
        pl.semaphore_signal(barrier, inc=1, device_id={"ctx": (c + off) % groups}, device_id_type=MESH)

    loads = [
        pltpu.make_async_copy(src, dst, lsem.at[i])
        for i, (src, dst) in enumerate([
            (gate_hbm, gate_ref), (route_hbm, route_ref), (d_hbm, d_ref), (q_hbm, q_ref), (g_hbm, g_ref),
            (k_hbm, k_ref), (v_hbm, v_ref), (s_hbm, s_ref),
        ])
    ]
    for load in loads:
        load.start()
    own = pltpu.make_async_copy(x_hbm, xall.at[s], xlocal)
    own.start()
    weights = [pltpu.make_async_copy(w_hbm.at[e], w_ref.at[e], wsem.at[e]) for e in range(experts)]
    for weight in weights:
        weight.start()
    loads[0].wait()
    loads[1].wait()
    top = gate_ref.shape[0]
    meta[s, 0:top] = gate_ref[...]
    meta[s, top:2 * top] = route_ref[...].astype(F32)

    pl.semaphore_wait(barrier, peers - 1 + groups - 1)

    def send_x(src, dst, slot, sem, to):
        return pltpu.make_async_remote_copy(
            src_ref=src, dst_ref=dst, send_sem=sem, recv_sem=xrecv.at[slot], device_id={"exp": to}, device_id_type=MESH
        )

    to_right = send_x(x_hbm, xall.at[s], s, xown.at[0], (s + 2) % peers)
    to_left = send_x(x_hbm, xall.at[s], s, xown.at[1], (s + peers - 2) % peers)
    to_sibling = send_x(x_hbm, xall.at[s], s, xown.at[2], sibling)

    @pl.when(z + 1 < line)
    def _():
        to_right.start()

    @pl.when(z >= 1)
    def _():
        to_left.start()

    to_sibling.start()

    metas = []
    for off in range(1, peers):
        metas.append(pltpu.make_async_remote_copy(
            src_ref=meta.at[s], dst_ref=meta.at[s], send_sem=msend.at[off], recv_sem=mrecv.at[s],
            device_id={"exp": (s + off) % peers}, device_id_type=MESH,
        ))
        metas[-1].start()

    def ways(d):
        left = (s + peers - 2 * d) % peers
        right = (s + 2 * d) % peers
        return (
            (left, z >= d, (s + 2) % peers, z + 1 < line),
            (right, z + d < line, (s + peers - 2) % peers, z >= 1),
        )

    def forwards(d, side):
        src, valid, onward, goes = ways(d)[side]
        on = send_x(xall.at[src], xall.at[src], src, xsend.at[(d - 1) * 4 + side * 2], onward)
        across = send_x(xall.at[src], xall.at[src], src, xsend.at[(d - 1) * 4 + side * 2 + 1], sibling)
        return src, valid, goes, on, across

    def relay(d):
        for side in range(2):
            src, valid, goes, on, across = forwards(d, side)

            @pl.when(valid)
            def _():
                across.wait_recv()

                @pl.when(goes)
                def _():
                    on.start()

                across.start()

    for load in loads[2:]:
        load.wait()
    rows = lax.broadcasted_iota(jnp.int32, (chunk, chunk), 0)
    cols = lax.broadcasted_iota(jnp.int32, (chunk, chunk), 1)
    lower = rows >= cols
    ones = jnp.where(lower, 1.0, 0.0).astype(BF16)
    ends, halves, ups, enlarged = [], [], [], []
    for a in range(count):
        part = pl.ds(a * chunk, chunk)
        cum = dot(ones, d_ref[part, :], 1, 0)
        end = cum[chunk - 1:chunk, :]
        up = jnp.exp(cum - 0.5 * end)
        ends.append(end)
        halves.append(jnp.exp(0.5 * end))
        ups.append(up)
        enl = split(q_ref[part, :].astype(F32) * up)
        enlarged.append(enl)
        mstate[a] = mm([g_ref[part, :]], enl, 0, 0) * halves[a]
        down = jnp.exp(0.5 * end - cum)
        ed_ref[part, :] = down
        red_ref[part, :] = k_ref[part, :].astype(F32) * down
    total = mstate[count - 1]
    for a in reversed(range(count - 1)):
        total = mstate[a] + jnp.exp(ends[a]) * total
    whole = ends[0]
    for a in range(1, count):
        whole = whole + ends[a]
    keys = message.shape[1]
    message[0:message.shape[0] - 8, :] = total
    message[message.shape[0] - 8:, :] = jnp.broadcast_to(jnp.exp(whole), (8, keys))

    def group_copy(d):
        return pltpu.make_async_remote_copy(
            src_ref=message, dst_ref=arrived.at[d - 1], send_sem=csend.at[d - 1], recv_sem=crecv.at[d - 1],
            device_id={"ctx": (c + groups - d) % groups}, device_id_type=MESH,
        )

    for d in range(1, groups):
        @pl.when(c >= d)
        def _():
            group_copy(d).start()

    if line > 1:
        relay(1)

    state = s_ref[...].T
    for a in range(count):
        part = pl.ds(a * chunk, chunk)
        g = g_ref[part, :]
        v = v_ref[part, :]
        red = split(red_ref[part, :])
        score = split(jnp.where(lower, dot(g, v, 1, 1), 0.0))
        flipped = split(jnp.where(rows <= cols, dot(v, g, 1, 1), 0.0))
        affinity = split(jnp.where(rows <= cols, mm(red, enlarged[a], 1, 1), 0.0))
        qg = mm([g], split(state * halves[a]), 1, 0) + mm(score, red, 1, 0)
        qg_ref[part, :] = (ups[a] * qg).astype(BF16)
        kpart[part, :] = mm(flipped, enlarged[a], 1, 0)
        vpart[part, :] = mm(affinity, [g], 1, 0)
        if a + 1 < count:
            state = jnp.exp(ends[a]) * state + mm([v], red, 0, 0) * halves[a]
    outs = [pltpu.make_async_copy(qg_ref, qg_hbm, osem.at[0])]
    outs[0].start()

    before = jnp.where(
        lax.broadcasted_iota(jnp.int32, (tokens, tokens), 0) < lax.broadcasted_iota(jnp.int32, (tokens, tokens), 1), 1.0, 0.0
    ).astype(BF16)

    def prepare(off, unused):
        src = (s + off) % peers

        @pl.when(off > 0)
        def _():
            pltpu.make_async_remote_copy(
                src_ref=meta.at[src], dst_ref=meta.at[src], send_sem=msend.at[0], recv_sem=mrecv.at[src],
                device_id={"exp": sibling}, device_id_type=MESH,
            ).wait_recv()

        gates = meta[src, 0:top]
        routes = meta[src, top:2 * top]
        first = (s * experts).astype(F32)
        place = lax.broadcasted_iota(jnp.int32, (MOST, tokens), 0).astype(F32)
        for e in range(experts):
            hit = routes == first + e
            member = jnp.sum(jnp.where(hit, 1.0, 0.0), axis=0, keepdims=True)
            gate = jnp.sum(jnp.where(hit, gates, 0.0), axis=0, keepdims=True)
            earlier = dot(jnp.broadcast_to(member, (8, tokens)).astype(BF16), before, 1, 0)[0:1]
            chosen = jnp.where(
                (jnp.broadcast_to(member, (MOST, tokens)) > 0.5) & (jnp.broadcast_to(earlier, (MOST, tokens)) == place), 1.0, 0.0
            )
            pick[src, e * MOST:(e + 1) * MOST, :] = chosen.astype(BF16)
            scale[src, e * MOST:(e + 1) * MOST, :] = jnp.broadcast_to(
                jnp.sum(chosen * gate, axis=1, keepdims=True), (MOST, scale.shape[2])
            )
        return unused

    lax.fori_loop(0, peers, prepare, 0)

    def build(src):
        rows_of = dot(pick[src], xall[src], 1, 0)
        scaled = (rows_of * scale[src][:, 0:1]).astype(BF16)
        for e in range(experts):
            slots[e, pl.ds(pl.multiple_of(src * MOST, MOST), MOST), :] = scaled[e * MOST:(e + 1) * MOST]

    if line > 2:
        relay(2)
    own.wait()
    build(s)
    send_x(xall.at[sibling], xall.at[sibling], sibling, xown.at[2], sibling).wait_recv()
    build(sibling)

    def finish(d):
        def one(i, unused):
            side = i // 2
            across = i % 2
            step = jnp.where(side == 0, peers - 2 * d, 2 * d)
            valid = jnp.where(side == 0, z >= d, z + d < line)
            mine = (s + step) % peers
            other = (mine // 2) * 2 + 1 - h
            src = jnp.where(across == 0, mine, other)

            @pl.when(valid)
            def _():
                @pl.when(across == 1)
                def _():
                    send_x(xall.at[src], xall.at[src], src, xown.at[2], sibling).wait_recv()

                build(src)

            return unused

        lax.fori_loop(0, 4, one, 0)

    if line > 1:
        finish(1)

    carry[...] = jnp.zeros_like(carry)
    for d in reversed(range(1, groups)):
        @pl.when(c + d < groups)
        def _():
            group_copy(d).wait_recv()
            size = carry.shape[0]
            carry[...] = arrived[d - 1, 0:size, :] + arrived[d - 1, size:size + 1, :] * carry[...]
    after = carry[...]
    for a in reversed(range(count)):
        part = pl.ds(a * chunk, chunk)
        later = split(after * halves[a])
        kg = kpart[part, :] + mm([v_ref[part, :]], later, 1, 0)
        kg_ref[part, :] = (ed_ref[part, :] * kg).astype(BF16)
        vg = vpart[part, :] + mm(split(red_ref[part, :]), later, 1, 1)
        vg_ref[part, :] = vg.astype(BF16)
        if a > 0:
            after = mstate[a] + jnp.exp(ends[a]) * after
    outs.append(pltpu.make_async_copy(kg_ref, kg_hbm, osem.at[1]))
    outs.append(pltpu.make_async_copy(vg_ref, vg_hbm, osem.at[2]))
    outs[1].start()
    outs[2].start()

    for d in range(2, line):
        if d > 2:
            relay(d)
        finish(d)

    for e in range(experts):
        weights[e].wait()
        product = dot(slots[e], w_ref[e], 1, 1).astype(BF16)
        for src in range(peers):
            out_ref[src, e] = product[src * MOST:(src + 1) * MOST]
        outs.append(pltpu.make_async_copy(out_ref.at[:, e], out_hbm.at[0, :, e], osem.at[3 + e]))
        outs[-1].start()

    @pl.when(z + 1 < line)
    def _():
        to_right.wait_send()

    @pl.when(z >= 1)
    def _():
        to_left.wait_send()

    to_sibling.wait_send()
    for copy in metas:
        copy.wait_send()
    for d in range(1, line):
        for side in range(2):
            src, valid, goes, on, across = forwards(d, side)

            @pl.when(valid)
            def _():
                @pl.when(goes)
                def _():
                    on.wait_send()

                across.wait_send()
    for d in range(1, groups):
        @pl.when(c >= d)
        def _():
            group_copy(d).wait_send()
    for copy in outs:
        copy.wait()


def local(
    query_heads, key_heads, value_heads, out_grad, log_decay, start_state, layer_grad, gate_weights, routes, expert_down
):
    groups = lax.axis_size("ctx")
    peers = lax.axis_size("exp")
    length, heads, keys = query_heads.shape
    values = value_heads.shape[2]
    tokens, width = layer_grad.shape
    top = routes.shape[1]
    experts, hidden, _ = expert_down.shape
    chunk = min(128, length)
    count = length // chunk
    line = peers // 2
    dma = pltpu.SemaphoreType.DMA
    hbm = pl.BlockSpec(memory_space=pl.ANY)
    qg, kg, vg, out = pl.pallas_call(
        functools.partial(kernel, groups, peers, chunk),
        out_shape=(
            jax.ShapeDtypeStruct((length, keys), BF16),
            jax.ShapeDtypeStruct((length, keys), BF16),
            jax.ShapeDtypeStruct((length, values), BF16),
            jax.ShapeDtypeStruct((1, peers, experts, MOST, hidden), BF16),
        ),
        in_specs=[hbm] * 10,
        out_specs=(hbm,) * 4,
        scratch_shapes=[
            pltpu.VMEM((length, keys), BF16),
            pltpu.VMEM((length, keys), BF16),
            pltpu.VMEM((length, values), BF16),
            pltpu.VMEM((length, values), BF16),
            pltpu.VMEM((length, keys), BF16),
            pltpu.VMEM((keys, values), F32),
            pltpu.VMEM((top, tokens), F32),
            pltpu.VMEM((top, tokens), jnp.int32),
            pltpu.VMEM((peers, 2 * top, tokens), F32),
            pltpu.VMEM((peers, tokens, width), BF16),
            pltpu.VMEM((experts, hidden, width), BF16),
            pltpu.VMEM((peers, experts * MOST, tokens), BF16),
            pltpu.VMEM((peers, experts * MOST, 128), F32),
            pltpu.VMEM((experts, peers * MOST, width), BF16),
            pltpu.VMEM((peers, experts, MOST, hidden), BF16),
            pltpu.VMEM((length, keys), BF16),
            pltpu.VMEM((length, keys), BF16),
            pltpu.VMEM((length, values), BF16),
            pltpu.VMEM((values + 8, keys), F32),
            pltpu.VMEM((max(1, groups - 1), values + 8, keys), F32),
            pltpu.VMEM((values, keys), F32),
            pltpu.VMEM((length, keys), F32),
            pltpu.VMEM((length, keys), F32),
            pltpu.VMEM((length, keys), F32),
            pltpu.VMEM((length, values), F32),
            pltpu.VMEM((count, values, keys), F32),
            dma((8,)),
            dma((experts,)),
            dma((3 + experts,)),
            dma((peers,)),
            dma((peers,)),
            dma((3,)),
            dma,
            dma((max(1, line - 1) * 4,)),
            dma((peers,)),
            dma((max(1, groups - 1),)),
            dma((max(1, groups - 1),)),
        ],
        compiler_params=pltpu.CompilerParams(
            collective_id=0, has_side_effects=True, vmem_limit_bytes=56 * 1024 * 1024
        ),
        cost_estimate=pl.CostEstimate(
            flops=2 * experts * peers * MOST * width * hidden, bytes_accessed=2 * experts * width * hidden, transcendentals=0
        ),
    )(
        query_heads[:, 0, :],
        key_heads[:, 0, :],
        value_heads[:, 0, :],
        out_grad[:, 0, :],
        log_decay[:, 0, :],
        start_state[0, 0],
        layer_grad,
        gate_weights.T,
        routes.T,
        expert_down,
    )
    return (
        qg.reshape(length, heads, keys),
        kg.reshape(length, heads, keys),
        vg.reshape(length, heads, values),
        out,
    )


def solution(mesh):
    return jax.shard_map(
        local,
        mesh=mesh,
        in_specs=(
            P("ctx", "exp", None),
            P("ctx", "exp", None),
            P("ctx", "exp", None),
            P("ctx", "exp", None),
            P("ctx", "exp", None),
            P("ctx", "exp", None, None),
            P(("ctx", "exp"), None),
            P(("ctx", "exp"), None),
            P(("ctx", "exp"), None),
            P("exp", None, None),
        ),
        out_specs=(
            P("ctx", "exp", None),
            P("ctx", "exp", None),
            P("ctx", "exp", None),
            P("ctx", None, "exp", None, None),
        ),
        check_vma=False,
    )
```

```python
import functools

import jax
import jax.numpy as jnp
from jax import lax
from jax.experimental import pallas as pl
from jax.experimental.pallas import tpu as pltpu
from jax.sharding import PartitionSpec as P

MOST = 16
F32 = jnp.float32
BF16 = jnp.bfloat16
MESH = pl.DeviceIdType.MESH


def dot(a, b, ca, cb):
    return lax.dot_general(a, b, (((ca,), (cb,)), ((), ())), preferred_element_type=F32)


def split(x):
    high = x.astype(BF16)
    return [high, (x - high.astype(F32)).astype(BF16)]


def mm(a, b, ca, cb):
    total = None
    for i, left in enumerate(a):
        for j, right in enumerate(b):
            if i + j < 2:
                term = dot(left, right, ca, cb)
                total = term if total is None else total + term
    return total


def kernel(
    groups, peers, chunk,
    q_hbm, k_hbm, v_hbm, g_hbm, d_hbm, s_hbm, x_hbm, gate_hbm, route_hbm, w_hbm,
    qg_ref, kg_ref, vg_ref, out_ref,
    q_ref, k_ref, v_ref, g_ref, d_ref, s_ref, gate_ref, route_ref, meta, xall, w_ref,
    pick, scale, slots, message, arrived, carry, ed_ref, red_ref,
    kpart, vpart, mstate, lsem, wsem, msend, mrecv, xown, xlocal, xsend, xrecv, csend, crecv,
):
    c = lax.axis_index("ctx")
    s = lax.axis_index("exp")
    z = s // 2
    h = s % 2
    line = peers // 2
    sibling = z * 2 + 1 - h
    length = q_ref.shape[0]
    count = length // chunk
    experts = w_ref.shape[0]
    tokens = xall.shape[1]

    barrier = pltpu.get_barrier_semaphore()
    for off in range(1, peers):
        pl.semaphore_signal(barrier, inc=1, device_id={"exp": (s + off) % peers}, device_id_type=MESH)
    for off in range(1, groups):
        pl.semaphore_signal(barrier, inc=1, device_id={"ctx": (c + off) % groups}, device_id_type=MESH)

    loads = [
        pltpu.make_async_copy(src, dst, lsem.at[i])
        for i, (src, dst) in enumerate([
            (gate_hbm, gate_ref), (route_hbm, route_ref), (d_hbm, d_ref), (q_hbm, q_ref), (g_hbm, g_ref),
            (k_hbm, k_ref), (v_hbm, v_ref), (s_hbm, s_ref),
        ])
    ]
    for load in loads:
        load.start()
    own = pltpu.make_async_copy(x_hbm, xall.at[s], xlocal)
    own.start()
    weights = [pltpu.make_async_copy(w_hbm.at[e], w_ref.at[e], wsem.at[e]) for e in range(experts)]
    for weight in weights:
        weight.start()
    loads[0].wait()
    loads[1].wait()
    top = gate_ref.shape[0]
    meta[s, 0:top] = gate_ref[...]
    meta[s, top:2 * top] = route_ref[...].astype(F32)

    pl.semaphore_wait(barrier, peers - 1 + groups - 1)

    def send_x(src, dst, slot, sem, to):
        return pltpu.make_async_remote_copy(
            src_ref=src, dst_ref=dst, send_sem=sem, recv_sem=xrecv.at[slot], device_id={"exp": to}, device_id_type=MESH
        )

    to_right = send_x(x_hbm, xall.at[s], s, xown.at[0], (s + 2) % peers)
    to_left = send_x(x_hbm, xall.at[s], s, xown.at[1], (s + peers - 2) % peers)
    to_sibling = send_x(x_hbm, xall.at[s], s, xown.at[2], sibling)

    @pl.when(z + 1 < line)
    def _():
        to_right.start()

    @pl.when(z >= 1)
    def _():
        to_left.start()

    to_sibling.start()

    metas = []
    for off in range(1, peers):
        metas.append(pltpu.make_async_remote_copy(
            src_ref=meta.at[s], dst_ref=meta.at[s], send_sem=msend.at[off], recv_sem=mrecv.at[s],
            device_id={"exp": (s + off) % peers}, device_id_type=MESH,
        ))
        metas[-1].start()

    def ways(d):
        left = (s + peers - 2 * d) % peers
        right = (s + 2 * d) % peers
        return (
            (left, z >= d, (s + 2) % peers, z + 1 < line),
            (right, z + d < line, (s + peers - 2) % peers, z >= 1),
        )

    def forwards(d, side):
        src, valid, onward, goes = ways(d)[side]
        on = send_x(xall.at[src], xall.at[src], src, xsend.at[(d - 1) * 4 + side * 2], onward)
        across = send_x(xall.at[src], xall.at[src], src, xsend.at[(d - 1) * 4 + side * 2 + 1], sibling)
        return src, valid, goes, on, across

    def relay(d):
        for side in range(2):
            src, valid, goes, on, across = forwards(d, side)

            @pl.when(valid)
            def _():
                across.wait_recv()

                @pl.when(goes)
                def _():
                    on.start()

                across.start()

    for load in loads[2:]:
        load.wait()
    rows = lax.broadcasted_iota(jnp.int32, (chunk, chunk), 0)
    cols = lax.broadcasted_iota(jnp.int32, (chunk, chunk), 1)
    lower = rows >= cols
    ones = jnp.where(lower, 1.0, 0.0).astype(BF16)
    ends, halves, ups, enlarged = [], [], [], []
    for a in range(count):
        part = pl.ds(a * chunk, chunk)
        cum = dot(ones, d_ref[part, :], 1, 0)
        end = cum[chunk - 1:chunk, :]
        up = jnp.exp(cum - 0.5 * end)
        ends.append(end)
        halves.append(jnp.exp(0.5 * end))
        ups.append(up)
        enl = split(q_ref[part, :].astype(F32) * up)
        enlarged.append(enl)
        mstate[a] = mm([g_ref[part, :]], enl, 0, 0) * halves[a]
        down = jnp.exp(0.5 * end - cum)
        ed_ref[part, :] = down
        red_ref[part, :] = k_ref[part, :].astype(F32) * down
    total = mstate[count - 1]
    for a in reversed(range(count - 1)):
        total = mstate[a] + jnp.exp(ends[a]) * total
    whole = ends[0]
    for a in range(1, count):
        whole = whole + ends[a]
    keys = message.shape[1]
    message[0:message.shape[0] - 8, :] = total
    message[message.shape[0] - 8:, :] = jnp.broadcast_to(jnp.exp(whole), (8, keys))

    def group_copy(d):
        return pltpu.make_async_remote_copy(
            src_ref=message, dst_ref=arrived.at[d - 1], send_sem=csend.at[d - 1], recv_sem=crecv.at[d - 1],
            device_id={"ctx": (c + groups - d) % groups}, device_id_type=MESH,
        )

    for d in range(1, groups):
        @pl.when(c >= d)
        def _():
            group_copy(d).start()

    if line > 1:
        relay(1)

    state = s_ref[...].T
    for a in range(count):
        part = pl.ds(a * chunk, chunk)
        g = g_ref[part, :]
        v = v_ref[part, :]
        red = split(red_ref[part, :])
        score = split(jnp.where(lower, dot(g, v, 1, 1), 0.0))
        flipped = split(jnp.where(rows <= cols, dot(v, g, 1, 1), 0.0))
        affinity = split(jnp.where(rows <= cols, mm(red, enlarged[a], 1, 1), 0.0))
        qg = mm([g], split(state * halves[a]), 1, 0) + mm(score, red, 1, 0)
        qg_ref[part, :] = (ups[a] * qg).astype(BF16)
        kpart[part, :] = mm(flipped, enlarged[a], 1, 0)
        vpart[part, :] = mm(affinity, [g], 1, 0)
        if a == 0 and line > 2:
            relay(2)
        if a + 1 < count:
            state = jnp.exp(ends[a]) * state + mm([v], red, 0, 0) * halves[a]

    before = jnp.where(
        lax.broadcasted_iota(jnp.int32, (tokens, tokens), 0) < lax.broadcasted_iota(jnp.int32, (tokens, tokens), 1), 1.0, 0.0
    ).astype(BF16)

    for off in range(1, peers):
        src = (s + off) % peers
        pltpu.make_async_remote_copy(
            src_ref=meta.at[src], dst_ref=meta.at[src], send_sem=msend.at[0], recv_sem=mrecv.at[src],
            device_id={"exp": sibling}, device_id_type=MESH,
        ).wait_recv()
    gates = meta[:, 0:top]
    routes = meta[:, top:2 * top]
    first = (s * experts).astype(F32)
    place = lax.broadcasted_iota(jnp.int32, (peers, MOST, tokens), 1).astype(F32)
    for e in range(experts):
        hit = routes == first + e
        member = jnp.sum(jnp.where(hit, 1.0, 0.0), axis=1)
        gate = jnp.sum(jnp.where(hit, gates, 0.0), axis=1)
        earlier = jnp.where(member > 0.5, dot(member.astype(BF16), before, 1, 0), -1.0)
        chosen = jnp.where(earlier[:, None, :] == place, 1.0, 0.0)
        pick[:, e * MOST:(e + 1) * MOST, :] = chosen.astype(BF16)
        weight = jnp.sum(chosen * gate[:, None, :], axis=2, keepdims=True)
        scale[:, e * MOST:(e + 1) * MOST, :] = jnp.broadcast_to(weight, (peers, MOST, scale.shape[2]))

    def build(src):
        rows_of = dot(pick[src], xall[src], 1, 0)
        scaled = (rows_of * scale[src][:, 0:1]).astype(BF16)
        for e in range(experts):
            slots[e, pl.ds(pl.multiple_of(src * MOST, MOST), MOST), :] = scaled[e * MOST:(e + 1) * MOST]

    own.wait()
    build(s)
    send_x(xall.at[sibling], xall.at[sibling], sibling, xown.at[2], sibling).wait_recv()
    build(sibling)

    def finish(d):
        def one(i, unused):
            side = i // 2
            across = i % 2
            step = jnp.where(side == 0, peers - 2 * d, 2 * d)
            valid = jnp.where(side == 0, z >= d, z + d < line)
            mine = (s + step) % peers
            other = (mine // 2) * 2 + 1 - h
            src = jnp.where(across == 0, mine, other)

            @pl.when(valid)
            def _():
                @pl.when(across == 1)
                def _():
                    send_x(xall.at[src], xall.at[src], src, xown.at[2], sibling).wait_recv()

                build(src)

            return unused

        lax.fori_loop(0, 4, one, 0)

    if line > 1:
        finish(1)

    carry[...] = jnp.zeros_like(carry)
    for d in reversed(range(1, groups)):
        @pl.when(c + d < groups)
        def _():
            group_copy(d).wait_recv()
            size = carry.shape[0]
            carry[...] = arrived[d - 1, 0:size, :] + arrived[d - 1, size:size + 1, :] * carry[...]
    after = carry[...]
    for a in reversed(range(count)):
        part = pl.ds(a * chunk, chunk)
        later = split(after * halves[a])
        kg = kpart[part, :] + mm([v_ref[part, :]], later, 1, 0)
        kg_ref[part, :] = (ed_ref[part, :] * kg).astype(BF16)
        vg = vpart[part, :] + mm(split(red_ref[part, :]), later, 1, 1)
        vg_ref[part, :] = vg.astype(BF16)
        if a > 0:
            after = mstate[a] + jnp.exp(ends[a]) * after

    for d in range(2, line):
        if d > 2:
            relay(d)
        finish(d)

    for e in range(experts):
        weights[e].wait()
        product = dot(slots[e], w_ref[e], 1, 1).astype(BF16)
        for src in range(peers):
            out_ref[0, src, e] = product[src * MOST:(src + 1) * MOST]

    @pl.when(z + 1 < line)
    def _():
        to_right.wait_send()

    @pl.when(z >= 1)
    def _():
        to_left.wait_send()

    to_sibling.wait_send()
    for copy in metas:
        copy.wait_send()
    for d in range(1, line):
        for side in range(2):
            src, valid, goes, on, across = forwards(d, side)

            @pl.when(valid)
            def _():
                @pl.when(goes)
                def _():
                    on.wait_send()

                across.wait_send()
    for d in range(1, groups):
        @pl.when(c >= d)
        def _():
            group_copy(d).wait_send()


def deliver(*refs):
    count = (len(refs) - 1) // 2
    sems = refs[-1]
    copies = [pltpu.make_async_copy(refs[i], refs[count + i], sems.at[i]) for i in range(count)]
    for copy in copies:
        copy.start()
    for copy in copies:
        copy.wait()


def local(
    query_heads, key_heads, value_heads, out_grad, log_decay, start_state, layer_grad, gate_weights, routes, expert_down
):
    groups = lax.axis_size("ctx")
    peers = lax.axis_size("exp")
    length, heads, keys = query_heads.shape
    values = value_heads.shape[2]
    tokens, width = layer_grad.shape
    top = routes.shape[1]
    experts, hidden, _ = expert_down.shape
    chunk = min(128, length)
    count = length // chunk
    line = peers // 2
    dma = pltpu.SemaphoreType.DMA
    hbm = pl.BlockSpec(memory_space=pl.ANY)
    shapes = ((length, keys), (length, keys), (length, values), (1, peers, experts, MOST, hidden))
    vmem = pl.BlockSpec(memory_space=pltpu.VMEM)
    held = pl.pallas_call(
        functools.partial(kernel, groups, peers, chunk),
        out_shape=tuple(pltpu.VMEM(shape, BF16) for shape in shapes),
        in_specs=[hbm] * 10,
        out_specs=(vmem,) * 4,
        scratch_shapes=[
            pltpu.VMEM((length, keys), BF16),
            pltpu.VMEM((length, keys), BF16),
            pltpu.VMEM((length, values), BF16),
            pltpu.VMEM((length, values), BF16),
            pltpu.VMEM((length, keys), BF16),
            pltpu.VMEM((keys, values), F32),
            pltpu.VMEM((top, tokens), F32),
            pltpu.VMEM((top, tokens), jnp.int32),
            pltpu.VMEM((peers, 2 * top, tokens), F32),
            pltpu.VMEM((peers, tokens, width), BF16),
            pltpu.VMEM((experts, hidden, width), BF16),
            pltpu.VMEM((peers, experts * MOST, tokens), BF16),
            pltpu.VMEM((peers, experts * MOST, 128), F32),
            pltpu.VMEM((experts, peers * MOST, width), BF16),
            pltpu.VMEM((values + 8, keys), F32),
            pltpu.VMEM((max(1, groups - 1), values + 8, keys), F32),
            pltpu.VMEM((values, keys), F32),
            pltpu.VMEM((length, keys), F32),
            pltpu.VMEM((length, keys), F32),
            pltpu.VMEM((length, keys), F32),
            pltpu.VMEM((length, values), F32),
            pltpu.VMEM((count, values, keys), F32),
            dma((8,)),
            dma((experts,)),
            dma((peers,)),
            dma((peers,)),
            dma((3,)),
            dma,
            dma((max(1, line - 1) * 4,)),
            dma((peers,)),
            dma((max(1, groups - 1),)),
            dma((max(1, groups - 1),)),
        ],
        compiler_params=pltpu.CompilerParams(
            collective_id=0, has_side_effects=True, vmem_limit_bytes=56 * 1024 * 1024
        ),
        cost_estimate=pl.CostEstimate(
            flops=2 * experts * peers * MOST * width * hidden, bytes_accessed=2 * experts * width * hidden, transcendentals=0
        ),
    )(
        query_heads[:, 0, :],
        key_heads[:, 0, :],
        value_heads[:, 0, :],
        out_grad[:, 0, :],
        log_decay[:, 0, :],
        start_state[0, 0],
        layer_grad,
        gate_weights.T,
        routes.T,
        expert_down,
    )
    qg, kg, vg, out = pl.pallas_call(
        deliver,
        out_shape=tuple(jax.ShapeDtypeStruct(shape, BF16) for shape in shapes),
        in_specs=[vmem] * 4,
        out_specs=(hbm,) * 4,
        scratch_shapes=[dma((4,))],
    )(*held)
    return (
        qg.reshape(length, heads, keys),
        kg.reshape(length, heads, keys),
        vg.reshape(length, heads, values),
        out,
    )


def solution(mesh):
    return jax.shard_map(
        local,
        mesh=mesh,
        in_specs=(
            P("ctx", "exp", None),
            P("ctx", "exp", None),
            P("ctx", "exp", None),
            P("ctx", "exp", None),
            P("ctx", "exp", None),
            P("ctx", "exp", None, None),
            P(("ctx", "exp"), None),
            P(("ctx", "exp"), None),
            P(("ctx", "exp"), None),
            P("exp", None, None),
        ),
        out_specs=(
            P("ctx", "exp", None),
            P("ctx", "exp", None),
            P("ctx", "exp", None),
            P("ctx", None, "exp", None, None),
        ),
        check_vma=False,
    )
```

```python
import functools

import jax
import jax.numpy as jnp
from jax import lax
from jax.experimental import pallas as pl
from jax.experimental.pallas import tpu as pltpu
from jax.sharding import PartitionSpec as P

MOST = 16
F32 = jnp.float32
BF16 = jnp.bfloat16
MESH = pl.DeviceIdType.MESH


def dot(a, b, ca, cb):
    return lax.dot_general(a, b, (((ca,), (cb,)), ((), ())), preferred_element_type=F32)


def split(x):
    high = x.astype(BF16)
    return [high, (x - high.astype(F32)).astype(BF16)]


def mm(a, b, ca, cb):
    total = None
    for i, left in enumerate(a):
        for j, right in enumerate(b):
            if i + j < 2:
                term = dot(left, right, ca, cb)
                total = term if total is None else total + term
    return total


def kernel(
    groups, peers, chunk, parts,
    q_hbm, k_hbm, v_hbm, g_hbm, d_hbm, s_hbm, x_hbm, gate_hbm, route_hbm, w_hbm,
    qg_ref, kg_ref, vg_ref, out_ref,
    q_ref, k_ref, v_ref, g_ref, d_ref, s_ref, gate_ref, route_ref, meta, xall, w_ref,
    pick, scale, slots, sums, message, arrived, carry, ed_ref, red_ref,
    kpart, vpart, mstate, lsem, wsem, msend, mrecv, xown, xlocal, xsend, xrecv, csend, crecv,
):
    c = lax.axis_index("ctx")
    s = lax.axis_index("exp")
    z = s // 2
    h = s % 2
    line = peers // 2
    sibling = z * 2 + 1 - h
    length = q_ref.shape[0]
    count = length // chunk
    experts = w_ref.shape[1]
    tokens = x_hbm.shape[0]
    wide = x_hbm.shape[1] // parts

    barrier = pltpu.get_barrier_semaphore()
    for off in range(1, peers):
        pl.semaphore_signal(barrier, inc=1, device_id={"exp": (s + off) % peers}, device_id_type=MESH)
    for off in range(1, groups):
        pl.semaphore_signal(barrier, inc=1, device_id={"ctx": (c + off) % groups}, device_id_type=MESH)

    loads = [
        pltpu.make_async_copy(src, dst, lsem.at[i])
        for i, (src, dst) in enumerate([
            (gate_hbm, gate_ref), (route_hbm, route_ref), (d_hbm, d_ref), (q_hbm, q_ref), (g_hbm, g_ref),
            (k_hbm, k_ref), (v_hbm, v_ref), (s_hbm, s_ref),
        ])
    ]
    for load in loads:
        load.start()
    def columns(p):
        return pl.ds(p * wide, wide)

    def block(p, src):
        return xall.at[p, pl.ds(pl.multiple_of(src * tokens, tokens), tokens)]

    own = [pltpu.make_async_copy(x_hbm.at[:, columns(p)], block(p, s), xlocal.at[p]) for p in range(parts)]
    for copy in own:
        copy.start()
    weights = [pltpu.make_async_copy(w_hbm.at[:, :, columns(p)], w_ref.at[p], wsem.at[p]) for p in range(parts)]
    for weight in weights:
        weight.start()
    loads[0].wait()
    loads[1].wait()
    top = gate_ref.shape[0]
    meta[s, 0:top] = gate_ref[...]
    meta[s, top:2 * top] = route_ref[...].astype(F32)

    pl.semaphore_wait(barrier, peers - 1 + groups - 1)

    def send_x(source, p, slot, sem, to):
        return pltpu.make_async_remote_copy(
            src_ref=source, dst_ref=block(p, slot), send_sem=sem, recv_sem=xrecv.at[p, slot],
            device_id={"exp": to}, device_id_type=MESH,
        )

    def firsts(p):
        mine = x_hbm.at[:, columns(p)]
        return (
            send_x(mine, p, s, xown.at[p, 0], (s + 2) % peers),
            send_x(mine, p, s, xown.at[p, 1], (s + peers - 2) % peers),
            send_x(mine, p, s, xown.at[p, 2], sibling),
        )

    for p in range(parts):
        to_right, to_left, to_sibling = firsts(p)

        @pl.when(z + 1 < line)
        def _():
            to_right.start()

        @pl.when(z >= 1)
        def _():
            to_left.start()

        to_sibling.start()

    metas = []
    for off in range(1, peers):
        metas.append(pltpu.make_async_remote_copy(
            src_ref=meta.at[s], dst_ref=meta.at[s], send_sem=msend.at[off], recv_sem=mrecv.at[s],
            device_id={"exp": (s + off) % peers}, device_id_type=MESH,
        ))
        metas[-1].start()

    def ways(d):
        left = (s + peers - 2 * d) % peers
        right = (s + 2 * d) % peers
        return (
            (left, z >= d, (s + 2) % peers, z + 1 < line),
            (right, z + d < line, (s + peers - 2) % peers, z >= 1),
        )

    def forwards(d, side, p):
        src, valid, onward, goes = ways(d)[side]
        row = (d - 1) * 4 + side * 2
        on = send_x(block(p, src), p, src, xsend.at[row, p], onward)
        across = send_x(block(p, src), p, src, xsend.at[row + 1, p], sibling)
        return src, valid, goes, on, across

    def relay(d, p):
        for side in range(2):
            src, valid, goes, on, across = forwards(d, side, p)

            @pl.when(valid)
            def _():
                across.wait_recv()

                @pl.when(goes)
                def _():
                    on.start()

                across.start()

    pending = [(d, p) for d in range(1, line) for p in range(parts)]

    def step():
        if pending:
            relay(*pending.pop(0))

    def ensure(d, p):
        while pending and pending[0] <= (d, p):
            step()

    for load in loads[2:]:
        load.wait()
    rows = lax.broadcasted_iota(jnp.int32, (chunk, chunk), 0)
    cols = lax.broadcasted_iota(jnp.int32, (chunk, chunk), 1)
    lower = rows >= cols
    ones = jnp.where(lower, 1.0, 0.0).astype(BF16)
    ends, halves, ups, enlarged = [], [], [], []
    for a in range(count):
        part = pl.ds(a * chunk, chunk)
        cum = dot(ones, d_ref[part, :], 1, 0)
        end = cum[chunk - 1:chunk, :]
        up = jnp.exp(cum - 0.5 * end)
        ends.append(end)
        halves.append(jnp.exp(0.5 * end))
        ups.append(up)
        enl = split(q_ref[part, :].astype(F32) * up)
        enlarged.append(enl)
        mstate[a] = mm([g_ref[part, :]], enl, 0, 0) * halves[a]
        down = jnp.exp(0.5 * end - cum)
        ed_ref[part, :] = down
        red_ref[part, :] = k_ref[part, :].astype(F32) * down
    total = mstate[count - 1]
    for a in reversed(range(count - 1)):
        total = mstate[a] + jnp.exp(ends[a]) * total
    whole = ends[0]
    for a in range(1, count):
        whole = whole + ends[a]
    keys = message.shape[1]
    message[0:message.shape[0] - 8, :] = total
    message[message.shape[0] - 8:, :] = jnp.broadcast_to(jnp.exp(whole), (8, keys))

    def group_copy(d):
        return pltpu.make_async_remote_copy(
            src_ref=message, dst_ref=arrived.at[d - 1], send_sem=csend.at[d - 1], recv_sem=crecv.at[d - 1],
            device_id={"ctx": (c + groups - d) % groups}, device_id_type=MESH,
        )

    for d in range(1, groups):
        @pl.when(c >= d)
        def _():
            group_copy(d).start()

    before = jnp.where(
        lax.broadcasted_iota(jnp.int32, (tokens, tokens), 0) < lax.broadcasted_iota(jnp.int32, (tokens, tokens), 1), 1.0, 0.0
    ).astype(BF16)
    for off in range(1, peers):
        src = (s + off) % peers
        pltpu.make_async_remote_copy(
            src_ref=meta.at[src], dst_ref=meta.at[src], send_sem=msend.at[0], recv_sem=mrecv.at[src],
            device_id={"exp": sibling}, device_id_type=MESH,
        ).wait_recv()
    gates = meta[:, 0:top]
    routes = meta[:, top:2 * top]
    first = (s * experts).astype(F32)
    place = lax.broadcasted_iota(jnp.int32, (peers, MOST, tokens), 1).astype(F32)
    pair = 2 * MOST
    core = lax.broadcasted_iota(jnp.int32, (line, pair, 2 * tokens), 1) // MOST
    mine = core == lax.broadcasted_iota(jnp.int32, (line, pair, 2 * tokens), 2) // tokens
    for e in range(experts):
        hit = routes == first + e
        member = jnp.sum(jnp.where(hit, 1.0, 0.0), axis=1)
        gate = jnp.sum(jnp.where(hit, gates, 0.0), axis=1)
        earlier = jnp.where(member > 0.5, dot(member.astype(BF16), before, 1, 0), -1.0)
        chosen = jnp.where(earlier[:, None, :] == place, 1.0, 0.0)
        weight = jnp.sum(chosen * gate[:, None, :], axis=2, keepdims=True).reshape(line, pair, 1)
        chosen = chosen.reshape(line, pair, tokens)
        chosen = jnp.where(mine, jnp.concatenate([chosen, chosen], axis=2), 0.0)
        pick[:, e * pair:(e + 1) * pair, :] = chosen.astype(BF16)
        scale[:, e * pair:(e + 1) * pair, :] = jnp.broadcast_to(weight, (line, pair, scale.shape[2]))

    def build(p, chip):
        picked = dot(pick[chip], xall[p, pl.ds(pl.multiple_of(chip * 2 * tokens, 2 * tokens), 2 * tokens), :], 1, 0)
        scaled = (picked * scale[chip][:, 0:1]).astype(BF16)
        for e in range(experts):
            slots[p, e, pl.ds(pl.multiple_of(chip * pair, pair), pair), :] = scaled[e * pair:(e + 1) * pair]

    def arrival(p, src):
        return send_x(block(p, src), p, src, xown.at[p, 2], sibling)

    def finish(d, p):
        ensure(d, p)
        for side in range(2):
            src, valid, onward, goes = ways(d)[side]

            @pl.when(valid)
            def _():
                arrival(p, (src // 2) * 2 + 1 - h).wait_recv()
                build(p, src // 2)

    step()
    for p in range(parts):
        own[p].wait()
        arrival(p, sibling).wait_recv()
        build(p, z)
    step()

    state = s_ref[...].T
    for a in range(count):
        part = pl.ds(a * chunk, chunk)
        g = g_ref[part, :]
        v = v_ref[part, :]
        red = split(red_ref[part, :])
        score = split(jnp.where(lower, dot(g, v, 1, 1), 0.0))
        flipped = split(jnp.where(rows <= cols, dot(v, g, 1, 1), 0.0))
        affinity = split(jnp.where(rows <= cols, mm(red, enlarged[a], 1, 1), 0.0))
        qg = mm([g], split(state * halves[a]), 1, 0) + mm(score, red, 1, 0)
        qg_ref[part, :] = (ups[a] * qg).astype(BF16)
        kpart[part, :] = mm(flipped, enlarged[a], 1, 0)
        vpart[part, :] = mm(affinity, [g], 1, 0)
        step()
        if a + 1 < count:
            state = jnp.exp(ends[a]) * state + mm([v], red, 0, 0) * halves[a]

    near = min(2, line)
    for d in range(1, near):
        for p in range(parts):
            finish(d, p)
            step()

    carry[...] = jnp.zeros_like(carry)
    for d in reversed(range(1, groups)):
        @pl.when(c + d < groups)
        def _():
            group_copy(d).wait_recv()
            size = carry.shape[0]
            carry[...] = arrived[d - 1, 0:size, :] + arrived[d - 1, size:size + 1, :] * carry[...]
    after = carry[...]
    for a in reversed(range(count)):
        part = pl.ds(a * chunk, chunk)
        later = split(after * halves[a])
        kg = kpart[part, :] + mm([v_ref[part, :]], later, 1, 0)
        kg_ref[part, :] = (ed_ref[part, :] * kg).astype(BF16)
        vg = vpart[part, :] + mm(split(red_ref[part, :]), later, 1, 1)
        vg_ref[part, :] = vg.astype(BF16)
        if a > 0:
            after = mstate[a] + jnp.exp(ends[a]) * after

    for p in range(parts):
        ensure(line - 1, min(p + 1, parts - 1))
        for d in range(near, line):
            finish(d, p)
        weights[p].wait()
        for e in range(experts):
            product = dot(slots[p, e], w_ref[p, e], 1, 1)
            if p > 0:
                product = product + sums[e]
            if p < parts - 1:
                sums[e] = product
            else:
                product = product.astype(BF16)
                for src in range(peers):
                    out_ref[0, src, e] = product[src * MOST:(src + 1) * MOST]

    for p in range(parts):
        to_right, to_left, to_sibling = firsts(p)

        @pl.when(z + 1 < line)
        def _():
            to_right.wait_send()

        @pl.when(z >= 1)
        def _():
            to_left.wait_send()

        to_sibling.wait_send()
    for copy in metas:
        copy.wait_send()
    for d in range(1, line):
        for p in range(parts):
            for side in range(2):
                src, valid, goes, on, across = forwards(d, side, p)

                @pl.when(valid)
                def _():
                    @pl.when(goes)
                    def _():
                        on.wait_send()

                    across.wait_send()
    for d in range(1, groups):
        @pl.when(c >= d)
        def _():
            group_copy(d).wait_send()


def deliver(*refs):
    count = (len(refs) - 1) // 2
    sems = refs[-1]
    copies = [pltpu.make_async_copy(refs[i], refs[count + i], sems.at[i]) for i in range(count)]
    for copy in copies:
        copy.start()
    for copy in copies:
        copy.wait()


def local(
    query_heads, key_heads, value_heads, out_grad, log_decay, start_state, layer_grad, gate_weights, routes, expert_down
):
    groups = lax.axis_size("ctx")
    peers = lax.axis_size("exp")
    length, heads, keys = query_heads.shape
    values = value_heads.shape[2]
    tokens, width = layer_grad.shape
    top = routes.shape[1]
    experts, hidden, _ = expert_down.shape
    chunk = min(128, length)
    count = length // chunk
    line = peers // 2
    parts = 3 if width % 384 == 0 else 1
    dma = pltpu.SemaphoreType.DMA
    hbm = pl.BlockSpec(memory_space=pl.ANY)
    shapes = ((length, keys), (length, keys), (length, values), (1, peers, experts, MOST, hidden))
    vmem = pl.BlockSpec(memory_space=pltpu.VMEM)
    held = pl.pallas_call(
        functools.partial(kernel, groups, peers, chunk, parts),
        out_shape=tuple(pltpu.VMEM(shape, BF16) for shape in shapes),
        in_specs=[hbm] * 10,
        out_specs=(vmem,) * 4,
        scratch_shapes=[
            pltpu.VMEM((length, keys), BF16),
            pltpu.VMEM((length, keys), BF16),
            pltpu.VMEM((length, values), BF16),
            pltpu.VMEM((length, values), BF16),
            pltpu.VMEM((length, keys), BF16),
            pltpu.VMEM((keys, values), F32),
            pltpu.VMEM((top, tokens), F32),
            pltpu.VMEM((top, tokens), jnp.int32),
            pltpu.VMEM((peers, 2 * top, tokens), F32),
            pltpu.VMEM((parts, peers * tokens, width // parts), BF16),
            pltpu.VMEM((parts, experts, hidden, width // parts), BF16),
            pltpu.VMEM((line, 2 * experts * MOST, 2 * tokens), BF16),
            pltpu.VMEM((line, 2 * experts * MOST, 128), F32),
            pltpu.VMEM((parts, experts, peers * MOST, width // parts), BF16),
            pltpu.VMEM((experts, peers * MOST, hidden), F32),
            pltpu.VMEM((values + 8, keys), F32),
            pltpu.VMEM((max(1, groups - 1), values + 8, keys), F32),
            pltpu.VMEM((values, keys), F32),
            pltpu.VMEM((length, keys), F32),
            pltpu.VMEM((length, keys), F32),
            pltpu.VMEM((length, keys), F32),
            pltpu.VMEM((length, values), F32),
            pltpu.VMEM((count, values, keys), F32),
            dma((8,)),
            dma((parts,)),
            dma((peers,)),
            dma((peers,)),
            dma((parts, 3)),
            dma((parts,)),
            dma((max(1, line - 1) * 4, parts)),
            dma((parts, peers)),
            dma((max(1, groups - 1),)),
            dma((max(1, groups - 1),)),
        ],
        compiler_params=pltpu.CompilerParams(
            collective_id=0, has_side_effects=True, vmem_limit_bytes=56 * 1024 * 1024
        ),
        cost_estimate=pl.CostEstimate(
            flops=2 * experts * peers * MOST * width * hidden, bytes_accessed=2 * experts * width * hidden, transcendentals=0
        ),
    )(
        query_heads[:, 0, :],
        key_heads[:, 0, :],
        value_heads[:, 0, :],
        out_grad[:, 0, :],
        log_decay[:, 0, :],
        start_state[0, 0],
        layer_grad,
        gate_weights.T,
        routes.T,
        expert_down,
    )
    qg, kg, vg, out = pl.pallas_call(
        deliver,
        out_shape=tuple(jax.ShapeDtypeStruct(shape, BF16) for shape in shapes),
        in_specs=[vmem] * 4,
        out_specs=(hbm,) * 4,
        scratch_shapes=[dma((4,))],
        compiler_params=pltpu.CompilerParams(vmem_limit_bytes=1024 * 1024),
    )(*held)
    return (
        qg.reshape(length, heads, keys),
        kg.reshape(length, heads, keys),
        vg.reshape(length, heads, values),
        out,
    )


def solution(mesh):
    return jax.shard_map(
        local,
        mesh=mesh,
        in_specs=(
            P("ctx", "exp", None),
            P("ctx", "exp", None),
            P("ctx", "exp", None),
            P("ctx", "exp", None),
            P("ctx", "exp", None),
            P("ctx", "exp", None, None),
            P(("ctx", "exp"), None),
            P(("ctx", "exp"), None),
            P(("ctx", "exp"), None),
            P("exp", None, None),
        ),
        out_specs=(
            P("ctx", "exp", None),
            P("ctx", "exp", None),
            P("ctx", "exp", None),
            P("ctx", None, "exp", None, None),
        ),
        check_vma=False,
    )
```

```python
import functools

import jax
import jax.numpy as jnp
from jax import lax
from jax.experimental import pallas as pl
from jax.experimental.pallas import tpu as pltpu
from jax.sharding import PartitionSpec as P

MOST = 16
F32 = jnp.float32
BF16 = jnp.bfloat16
MESH = pl.DeviceIdType.MESH


def dot(a, b, ca, cb):
    return lax.dot_general(a, b, (((ca,), (cb,)), ((), ())), preferred_element_type=F32)


def split(x):
    high = x.astype(BF16)
    return [high, (x - high.astype(F32)).astype(BF16)]


def mm(a, b, ca, cb):
    total = None
    for i, left in enumerate(a):
        for j, right in enumerate(b):
            if i + j < 2:
                term = dot(left, right, ca, cb)
                total = term if total is None else total + term
    return total


def kernel(
    groups, peers, chunk, parts,
    q_hbm, k_hbm, v_hbm, g_hbm, d_hbm, s_hbm, x_hbm, gate_hbm, route_hbm, w_hbm,
    qg_ref, kg_ref, vg_ref, out_ref,
    q_ref, k_ref, v_ref, g_ref, d_ref, s_ref, gate_ref, route_ref, meta, xall, w_ref,
    pick, scale, slots, sums, message, arrived, carry, ed_ref, red_ref,
    kpart, vpart, mstate, lsem, wsem, msend, mrecv, xown, xlocal, xsend, xrecv, csend, crecv,
):
    c = lax.axis_index("ctx")
    s = lax.axis_index("exp")
    z = s // 2
    h = s % 2
    line = peers // 2
    sibling = z * 2 + 1 - h
    length = q_ref.shape[0]
    count = length // chunk
    experts = w_ref.shape[1]
    tokens = x_hbm.shape[0]
    wide = x_hbm.shape[1] // parts

    barrier = pltpu.get_barrier_semaphore()
    for off in range(1, peers):
        pl.semaphore_signal(barrier, inc=1, device_id={"exp": (s + off) % peers}, device_id_type=MESH)
    for off in range(1, groups):
        pl.semaphore_signal(barrier, inc=1, device_id={"ctx": (c + off) % groups}, device_id_type=MESH)

    loads = [
        pltpu.make_async_copy(src, dst, lsem.at[i])
        for i, (src, dst) in enumerate([
            (gate_hbm, gate_ref), (route_hbm, route_ref), (d_hbm, d_ref), (q_hbm, q_ref), (g_hbm, g_ref),
            (k_hbm, k_ref), (v_hbm, v_ref), (s_hbm, s_ref),
        ])
    ]
    for load in loads:
        load.start()
    def columns(p):
        return pl.ds(p * wide, wide)

    def block(p, src):
        return xall.at[p, pl.ds(pl.multiple_of(src * tokens, tokens), tokens)]

    own = [pltpu.make_async_copy(x_hbm.at[:, columns(p)], block(p, s), xlocal.at[p]) for p in range(parts)]
    for copy in own:
        copy.start()
    weights = [pltpu.make_async_copy(w_hbm.at[:, :, columns(p)], w_ref.at[p], wsem.at[p]) for p in range(parts)]
    for weight in weights:
        weight.start()
    loads[0].wait()
    loads[1].wait()
    top = gate_ref.shape[0]
    meta[s, 0:top] = gate_ref[...]
    meta[s, top:2 * top] = route_ref[...].astype(F32)

    pl.semaphore_wait(barrier, peers - 1 + groups - 1)

    def send_x(source, p, slot, sem, to):
        return pltpu.make_async_remote_copy(
            src_ref=source, dst_ref=block(p, slot), send_sem=sem, recv_sem=xrecv.at[p, slot],
            device_id={"exp": to}, device_id_type=MESH,
        )

    def ways(d):
        return ((s + peers - 2 * d) % peers, z >= d), ((s + 2 * d) % peers, z + d < line)

    def outgoing(p):
        mine = x_hbm.at[:, columns(p)]
        for d in reversed(range(1, line)):
            for side, (to, valid) in enumerate(ways(d)):
                yield valid, send_x(mine, p, s, xsend.at[(d - 1) * 4 + side * 2, p], to)

    def incoming(p):
        for d in range(1, line):
            for side, (src, valid) in enumerate(ways(d)):
                yield src, valid, send_x(block(p, src), p, src, xsend.at[(d - 1) * 4 + side * 2 + 1, p], sibling)

    beside = [send_x(x_hbm.at[:, columns(p)], p, s, xown.at[p], sibling) for p in range(parts)]
    for p in range(parts):
        for valid, copy in outgoing(p):
            @pl.when(valid)
            def _():
                copy.start()

        beside[p].start()

    metas = []
    for off in range(1, peers):
        metas.append(pltpu.make_async_remote_copy(
            src_ref=meta.at[s], dst_ref=meta.at[s], send_sem=msend.at[off], recv_sem=mrecv.at[s],
            device_id={"exp": (s + off) % peers}, device_id_type=MESH,
        ))
        metas[-1].start()

    def relay(p):
        for src, valid, copy in incoming(p):
            @pl.when(valid)
            def _():
                copy.wait_recv()
                copy.start()

    for load in loads[2:]:
        load.wait()
    rows = lax.broadcasted_iota(jnp.int32, (chunk, chunk), 0)
    cols = lax.broadcasted_iota(jnp.int32, (chunk, chunk), 1)
    lower = rows >= cols
    ones = jnp.where(lower, 1.0, 0.0).astype(BF16)
    ends, halves, ups, enlarged = [], [], [], []
    for a in range(count):
        part = pl.ds(a * chunk, chunk)
        cum = dot(ones, d_ref[part, :], 1, 0)
        end = cum[chunk - 1:chunk, :]
        up = jnp.exp(cum - 0.5 * end)
        ends.append(end)
        halves.append(jnp.exp(0.5 * end))
        ups.append(up)
        enl = split(q_ref[part, :].astype(F32) * up)
        enlarged.append(enl)
        mstate[a] = mm([g_ref[part, :]], enl, 0, 0) * halves[a]
        down = jnp.exp(0.5 * end - cum)
        ed_ref[part, :] = down
        red_ref[part, :] = k_ref[part, :].astype(F32) * down
    total = mstate[count - 1]
    for a in reversed(range(count - 1)):
        total = mstate[a] + jnp.exp(ends[a]) * total
    whole = ends[0]
    for a in range(1, count):
        whole = whole + ends[a]
    keys = message.shape[1]
    message[0:message.shape[0] - 8, :] = total
    message[message.shape[0] - 8:, :] = jnp.broadcast_to(jnp.exp(whole), (8, keys))

    def group_copy(d):
        return pltpu.make_async_remote_copy(
            src_ref=message, dst_ref=arrived.at[d - 1], send_sem=csend.at[d - 1], recv_sem=crecv.at[d - 1],
            device_id={"ctx": (c + groups - d) % groups}, device_id_type=MESH,
        )

    for d in range(1, groups):
        @pl.when(c >= d)
        def _():
            group_copy(d).start()

    before = jnp.where(
        lax.broadcasted_iota(jnp.int32, (tokens, tokens), 0) < lax.broadcasted_iota(jnp.int32, (tokens, tokens), 1), 1.0, 0.0
    ).astype(BF16)
    for off in range(1, peers):
        src = (s + off) % peers
        pltpu.make_async_remote_copy(
            src_ref=meta.at[src], dst_ref=meta.at[src], send_sem=msend.at[0], recv_sem=mrecv.at[src],
            device_id={"exp": sibling}, device_id_type=MESH,
        ).wait_recv()
    gates = meta[:, 0:top]
    routes = meta[:, top:2 * top]
    first = (s * experts).astype(F32)
    place = lax.broadcasted_iota(jnp.int32, (peers, MOST, tokens), 1).astype(F32)
    pair = 2 * MOST
    core = lax.broadcasted_iota(jnp.int32, (line, pair, 2 * tokens), 1) // MOST
    mine = core == lax.broadcasted_iota(jnp.int32, (line, pair, 2 * tokens), 2) // tokens
    for e in range(experts):
        hit = routes == first + e
        member = jnp.sum(jnp.where(hit, 1.0, 0.0), axis=1)
        gate = jnp.sum(jnp.where(hit, gates, 0.0), axis=1)
        earlier = jnp.where(member > 0.5, dot(member.astype(BF16), before, 1, 0), -1.0)
        chosen = jnp.where(earlier[:, None, :] == place, 1.0, 0.0)
        weight = jnp.sum(chosen * gate[:, None, :], axis=2, keepdims=True).reshape(line, pair, 1)
        chosen = chosen.reshape(line, pair, tokens)
        chosen = jnp.where(mine, jnp.concatenate([chosen, chosen], axis=2), 0.0)
        pick[:, e * pair:(e + 1) * pair, :] = chosen.astype(BF16)
        scale[:, e * pair:(e + 1) * pair, :] = jnp.broadcast_to(weight, (line, pair, scale.shape[2]))

    def build(p, chip):
        picked = dot(pick[chip], xall[p, pl.ds(pl.multiple_of(chip * 2 * tokens, 2 * tokens), 2 * tokens), :], 1, 0)
        scaled = (picked * scale[chip][:, 0:1]).astype(BF16)
        for e in range(experts):
            slots[p, e, pl.ds(pl.multiple_of(chip * pair, pair), pair), :] = scaled[e * pair:(e + 1) * pair]

    def arrival(p, src):
        return send_x(block(p, src), p, src, xown.at[p], sibling)

    def finish(p):
        for src, valid in [way for d in range(1, line) for way in ways(d)]:
            @pl.when(valid)
            def _():
                arrival(p, (src // 2) * 2 + 1 - h).wait_recv()
                build(p, src // 2)

    def multiply(p):
        weights[p].wait()
        for e in range(experts):
            product = dot(w_ref[p, e], slots[p, e], 1, 1)
            if p > 0:
                product = product + sums[e]
            if p < parts - 1:
                sums[e] = product
            else:
                product = product.T.astype(BF16)
                for src in range(peers):
                    out_ref[0, src, e] = product[src * MOST:(src + 1) * MOST]

    for p in range(parts):
        own[p].wait()
        arrival(p, sibling).wait_recv()
        build(p, z)

    def attend(a, state):
        part = pl.ds(a * chunk, chunk)
        g = g_ref[part, :]
        v = v_ref[part, :]
        red = split(red_ref[part, :])
        score = split(jnp.where(lower, dot(g, v, 1, 1), 0.0))
        flipped = split(jnp.where(rows <= cols, dot(v, g, 1, 1), 0.0))
        affinity = split(jnp.where(rows <= cols, mm(red, enlarged[a], 1, 1), 0.0))
        qg = mm([g], split(state * halves[a]), 1, 0) + mm(score, red, 1, 0)
        qg_ref[part, :] = (ups[a] * qg).astype(BF16)
        kpart[part, :] = mm(flipped, enlarged[a], 1, 0)
        vpart[part, :] = mm(affinity, [g], 1, 0)
        if a + 1 < count:
            state = jnp.exp(ends[a]) * state + mm([v], red, 0, 0) * halves[a]
        return state

    def adjoin():
        carry[...] = jnp.zeros_like(carry)
        for d in reversed(range(1, groups)):
            @pl.when(c + d < groups)
            def _():
                group_copy(d).wait_recv()
                size = carry.shape[0]
                carry[...] = arrived[d - 1, 0:size, :] + arrived[d - 1, size:size + 1, :] * carry[...]
        after = carry[...]
        for a in reversed(range(count)):
            part = pl.ds(a * chunk, chunk)
            later = split(after * halves[a])
            kg = kpart[part, :] + mm([v_ref[part, :]], later, 1, 0)
            kg_ref[part, :] = (ed_ref[part, :] * kg).astype(BF16)
            vg = vpart[part, :] + mm(split(red_ref[part, :]), later, 1, 1)
            vg_ref[part, :] = vg.astype(BF16)
            if a > 0:
                after = mstate[a] + jnp.exp(ends[a]) * after

    state = s_ref[...].T
    turn = 0
    for p in range(parts):
        relay(p)
        while turn < count and (turn <= p or p == parts - 1):
            state = attend(turn, state)
            turn += 1
        if p == parts - 1:
            adjoin()
        finish(p)
        multiply(p)

    for p in range(parts):
        for valid, copy in outgoing(p):
            @pl.when(valid)
            def _():
                copy.wait_send()

        beside[p].wait_send()
        for src, valid, copy in incoming(p):
            @pl.when(valid)
            def _():
                copy.wait_send()
    for copy in metas:
        copy.wait_send()
    for d in range(1, groups):
        @pl.when(c >= d)
        def _():
            group_copy(d).wait_send()


def deliver(*refs):
    count = (len(refs) - 1) // 2
    sems = refs[-1]
    copies = [pltpu.make_async_copy(refs[i], refs[count + i], sems.at[i]) for i in range(count)]
    for copy in copies:
        copy.start()
    for copy in copies:
        copy.wait()


def local(
    query_heads, key_heads, value_heads, out_grad, log_decay, start_state, layer_grad, gate_weights, routes, expert_down
):
    groups = lax.axis_size("ctx")
    peers = lax.axis_size("exp")
    length, heads, keys = query_heads.shape
    values = value_heads.shape[2]
    tokens, width = layer_grad.shape
    top = routes.shape[1]
    experts, hidden, _ = expert_down.shape
    chunk = min(128, length)
    count = length // chunk
    line = peers // 2
    parts = 3 if width % 384 == 0 else 1
    dma = pltpu.SemaphoreType.DMA
    hbm = pl.BlockSpec(memory_space=pl.ANY)
    shapes = ((length, keys), (length, keys), (length, values), (1, peers, experts, MOST, hidden))
    vmem = pl.BlockSpec(memory_space=pltpu.VMEM)
    held = pl.pallas_call(
        functools.partial(kernel, groups, peers, chunk, parts),
        out_shape=tuple(pltpu.VMEM(shape, BF16) for shape in shapes),
        in_specs=[hbm] * 10,
        out_specs=(vmem,) * 4,
        scratch_shapes=[
            pltpu.VMEM((length, keys), BF16),
            pltpu.VMEM((length, keys), BF16),
            pltpu.VMEM((length, values), BF16),
            pltpu.VMEM((length, values), BF16),
            pltpu.VMEM((length, keys), BF16),
            pltpu.VMEM((keys, values), F32),
            pltpu.VMEM((top, tokens), F32),
            pltpu.VMEM((top, tokens), jnp.int32),
            pltpu.VMEM((peers, 2 * top, tokens), F32),
            pltpu.VMEM((parts, peers * tokens, width // parts), BF16),
            pltpu.VMEM((parts, experts, hidden, width // parts), BF16),
            pltpu.VMEM((line, 2 * experts * MOST, 2 * tokens), BF16),
            pltpu.VMEM((line, 2 * experts * MOST, 128), F32),
            pltpu.VMEM((parts, experts, peers * MOST, width // parts), BF16),
            pltpu.VMEM((experts, hidden, peers * MOST), F32),
            pltpu.VMEM((values + 8, keys), F32),
            pltpu.VMEM((max(1, groups - 1), values + 8, keys), F32),
            pltpu.VMEM((values, keys), F32),
            pltpu.VMEM((length, keys), F32),
            pltpu.VMEM((length, keys), F32),
            pltpu.VMEM((length, keys), F32),
            pltpu.VMEM((length, values), F32),
            pltpu.VMEM((count, values, keys), F32),
            dma((8,)),
            dma((parts,)),
            dma((peers,)),
            dma((peers,)),
            dma((parts,)),
            dma((parts,)),
            dma((max(1, line - 1) * 4, parts)),
            dma((parts, peers)),
            dma((max(1, groups - 1),)),
            dma((max(1, groups - 1),)),
        ],
        compiler_params=pltpu.CompilerParams(
            collective_id=0, has_side_effects=True, vmem_limit_bytes=56 * 1024 * 1024
        ),
        cost_estimate=pl.CostEstimate(
            flops=2 * experts * peers * MOST * width * hidden, bytes_accessed=2 * experts * width * hidden, transcendentals=0
        ),
    )(
        query_heads[:, 0, :],
        key_heads[:, 0, :],
        value_heads[:, 0, :],
        out_grad[:, 0, :],
        log_decay[:, 0, :],
        start_state[0, 0],
        layer_grad,
        gate_weights.T,
        routes.T,
        expert_down,
    )
    qg, kg, vg, out = pl.pallas_call(
        deliver,
        out_shape=tuple(jax.ShapeDtypeStruct(shape, BF16) for shape in shapes),
        in_specs=[vmem] * 4,
        out_specs=(hbm,) * 4,
        scratch_shapes=[dma((4,))],
        compiler_params=pltpu.CompilerParams(vmem_limit_bytes=1024 * 1024),
    )(*held)
    return (
        qg.reshape(length, heads, keys),
        kg.reshape(length, heads, keys),
        vg.reshape(length, heads, values),
        out,
    )


def solution(mesh):
    return jax.shard_map(
        local,
        mesh=mesh,
        in_specs=(
            P("ctx", "exp", None),
            P("ctx", "exp", None),
            P("ctx", "exp", None),
            P("ctx", "exp", None),
            P("ctx", "exp", None),
            P("ctx", "exp", None, None),
            P(("ctx", "exp"), None),
            P(("ctx", "exp"), None),
            P(("ctx", "exp"), None),
            P("exp", None, None),
        ),
        out_specs=(
            P("ctx", "exp", None),
            P("ctx", "exp", None),
            P("ctx", "exp", None),
            P("ctx", None, "exp", None, None),
        ),
        check_vma=False,
    )
```

```python
import functools

import jax
import jax.numpy as jnp
from jax import lax
from jax.experimental import pallas as pl
from jax.experimental.pallas import tpu as pltpu
from jax.sharding import PartitionSpec as P

MOST = 16
F32 = jnp.float32
BF16 = jnp.bfloat16
MESH = pl.DeviceIdType.MESH


def dot(a, b, ca, cb):
    return lax.dot_general(a, b, (((ca,), (cb,)), ((), ())), preferred_element_type=F32)


def split(x):
    high = x.astype(BF16)
    return [high, (x - high.astype(F32)).astype(BF16)]


def mm(a, b, ca, cb):
    total = None
    for i, left in enumerate(a):
        for j, right in enumerate(b):
            if i + j < 2:
                term = dot(left, right, ca, cb)
                total = term if total is None else total + term
    return total


def kernel(
    groups, peers, chunk, parts,
    q_hbm, k_hbm, v_hbm, g_hbm, d_hbm, s_hbm, x_hbm, gate_hbm, route_hbm, w_hbm,
    qg_ref, kg_ref, vg_ref, out_ref,
    q_ref, k_ref, v_ref, g_ref, d_ref, s_ref, gate_ref, route_ref, meta, xall, w_ref,
    pick, scale, slots, sums, message, arrived, carry, ed_ref, red_ref,
    kpart, vpart, mstate, lsem, wsem, msend, mrecv, xown, xlocal, xsend, xrecv, csend, crecv,
):
    c = lax.axis_index("ctx")
    s = lax.axis_index("exp")
    z = s // 2
    h = s % 2
    line = peers // 2
    sibling = z * 2 + 1 - h
    length = q_ref.shape[0]
    count = length // chunk
    experts = w_ref.shape[1]
    tokens = x_hbm.shape[0]
    wide = x_hbm.shape[1] // parts

    barrier = pltpu.get_barrier_semaphore()
    for off in range(1, peers):
        pl.semaphore_signal(barrier, inc=1, device_id={"exp": (s + off) % peers}, device_id_type=MESH)
    for off in range(1, groups):
        pl.semaphore_signal(barrier, inc=1, device_id={"ctx": (c + off) % groups}, device_id_type=MESH)

    loads = [
        pltpu.make_async_copy(src, dst, lsem.at[i])
        for i, (src, dst) in enumerate([
            (gate_hbm, gate_ref), (route_hbm, route_ref), (d_hbm, d_ref), (q_hbm, q_ref), (g_hbm, g_ref),
            (k_hbm, k_ref), (v_hbm, v_ref), (s_hbm, s_ref),
        ])
    ]
    for load in loads:
        load.start()
    def columns(p):
        return pl.ds(p * wide, wide)

    def block(p, src):
        return xall.at[p, pl.ds(pl.multiple_of(src * tokens, tokens), tokens)]

    own = [pltpu.make_async_copy(x_hbm.at[:, columns(p)], block(p, s), xlocal.at[p]) for p in range(parts)]
    for copy in own:
        copy.start()
    weights = [pltpu.make_async_copy(w_hbm.at[:, :, columns(p)], w_ref.at[p], wsem.at[p]) for p in range(parts)]
    for weight in weights:
        weight.start()
    loads[0].wait()
    loads[1].wait()
    top = gate_ref.shape[0]
    meta[s, 0:top] = gate_ref[...]
    meta[s, top:2 * top] = route_ref[...].astype(F32)

    pl.semaphore_wait(barrier, peers - 1 + groups - 1)

    def send_x(source, p, slot, sem, to):
        return pltpu.make_async_remote_copy(
            src_ref=source, dst_ref=block(p, slot), send_sem=sem, recv_sem=xrecv.at[p, slot],
            device_id={"exp": to}, device_id_type=MESH,
        )

    def firsts(p):
        mine = x_hbm.at[:, columns(p)]
        return (
            send_x(mine, p, s, xown.at[p, 0], (s + 2) % peers),
            send_x(mine, p, s, xown.at[p, 1], (s + peers - 2) % peers),
            send_x(mine, p, s, xown.at[p, 2], sibling),
        )

    for p in range(parts):
        to_right, to_left, to_sibling = firsts(p)

        @pl.when(z + 1 < line)
        def _():
            to_right.start()

        @pl.when(z >= 1)
        def _():
            to_left.start()

        to_sibling.start()

    metas = []
    for off in range(1, peers):
        metas.append(pltpu.make_async_remote_copy(
            src_ref=meta.at[s], dst_ref=meta.at[s], send_sem=msend.at[off], recv_sem=mrecv.at[s],
            device_id={"exp": (s + off) % peers}, device_id_type=MESH,
        ))
        metas[-1].start()

    def ways(d):
        left = (s + peers - 2 * d) % peers
        right = (s + 2 * d) % peers
        return (
            (left, z >= d, (s + 2) % peers, z + 1 < line),
            (right, z + d < line, (s + peers - 2) % peers, z >= 1),
        )

    def forwards(d, side, p):
        src, valid, onward, goes = ways(d)[side]
        row = (d - 1) * 4 + side * 2
        on = send_x(block(p, src), p, src, xsend.at[row, p], onward)
        across = send_x(block(p, src), p, src, xsend.at[row + 1, p], sibling)
        return src, valid, goes, on, across

    def relay(d, p):
        for side in range(2):
            src, valid, goes, on, across = forwards(d, side, p)

            @pl.when(valid)
            def _():
                across.wait_recv()

                @pl.when(goes)
                def _():
                    on.start()

                across.start()

    pending = [(d, p) for d in range(1, line) for p in range(parts)]

    def step():
        if pending:
            relay(*pending.pop(0))

    def ensure(d, p):
        while pending and pending[0] <= (d, p):
            step()

    for load in loads[2:]:
        load.wait()
    rows = lax.broadcasted_iota(jnp.int32, (chunk, chunk), 0)
    cols = lax.broadcasted_iota(jnp.int32, (chunk, chunk), 1)
    lower = rows >= cols
    ones = jnp.where(lower, 1.0, 0.0).astype(BF16)
    ends, halves, ups, enlarged = [], [], [], []
    for a in range(count):
        part = pl.ds(a * chunk, chunk)
        cum = dot(ones, d_ref[part, :], 1, 0)
        end = cum[chunk - 1:chunk, :]
        up = jnp.exp(cum - 0.5 * end)
        ends.append(end)
        halves.append(jnp.exp(0.5 * end))
        ups.append(up)
        enl = split(q_ref[part, :].astype(F32) * up)
        enlarged.append(enl)
        mstate[a] = mm([g_ref[part, :]], enl, 0, 0) * halves[a]
        down = jnp.exp(0.5 * end - cum)
        ed_ref[part, :] = down
        red_ref[part, :] = k_ref[part, :].astype(F32) * down
    total = mstate[count - 1]
    for a in reversed(range(count - 1)):
        total = mstate[a] + jnp.exp(ends[a]) * total
    whole = ends[0]
    for a in range(1, count):
        whole = whole + ends[a]
    keys = message.shape[1]
    message[0:message.shape[0] - 8, :] = total
    message[message.shape[0] - 8:, :] = jnp.broadcast_to(jnp.exp(whole), (8, keys))

    def group_copy(d):
        return pltpu.make_async_remote_copy(
            src_ref=message, dst_ref=arrived.at[d - 1], send_sem=csend.at[d - 1], recv_sem=crecv.at[d - 1],
            device_id={"ctx": (c + groups - d) % groups}, device_id_type=MESH,
        )

    for d in range(1, groups):
        @pl.when(c >= d)
        def _():
            group_copy(d).start()

    before = jnp.where(
        lax.broadcasted_iota(jnp.int32, (tokens, tokens), 0) < lax.broadcasted_iota(jnp.int32, (tokens, tokens), 1), 1.0, 0.0
    ).astype(BF16)
    for off in range(1, peers):
        src = (s + off) % peers
        pltpu.make_async_remote_copy(
            src_ref=meta.at[src], dst_ref=meta.at[src], send_sem=msend.at[0], recv_sem=mrecv.at[src],
            device_id={"exp": sibling}, device_id_type=MESH,
        ).wait_recv()
    gates = meta[:, 0:top]
    routes = meta[:, top:2 * top]
    first = (s * experts).astype(F32)
    place = lax.broadcasted_iota(jnp.int32, (peers, MOST, tokens), 1).astype(F32)
    pair = 2 * MOST
    core = lax.broadcasted_iota(jnp.int32, (line, pair, 2 * tokens), 1) // MOST
    mine = core == lax.broadcasted_iota(jnp.int32, (line, pair, 2 * tokens), 2) // tokens
    for e in range(experts):
        hit = routes == first + e
        member = jnp.sum(jnp.where(hit, 1.0, 0.0), axis=1)
        gate = jnp.sum(jnp.where(hit, gates, 0.0), axis=1)
        earlier = jnp.where(member > 0.5, dot(member.astype(BF16), before, 1, 0), -1.0)
        chosen = jnp.where(earlier[:, None, :] == place, 1.0, 0.0)
        weight = jnp.sum(chosen * gate[:, None, :], axis=2, keepdims=True).reshape(line, pair, 1)
        chosen = chosen.reshape(line, pair, tokens)
        chosen = jnp.where(mine, jnp.concatenate([chosen, chosen], axis=2), 0.0)
        pick[:, e * pair:(e + 1) * pair, :] = chosen.astype(BF16)
        scale[:, e * pair:(e + 1) * pair, :] = jnp.broadcast_to(weight, (line, pair, scale.shape[2]))

    def build(p, chip):
        picked = dot(pick[chip], xall[p, pl.ds(pl.multiple_of(chip * 2 * tokens, 2 * tokens), 2 * tokens), :], 1, 0)
        scaled = (picked * scale[chip][:, 0:1]).astype(BF16)
        for e in range(experts):
            slots[p, e, pl.ds(pl.multiple_of(chip * pair, pair), pair), :] = scaled[e * pair:(e + 1) * pair]

    def arrival(p, src):
        return send_x(block(p, src), p, src, xown.at[p, 2], sibling)

    def finish(d, p):
        ensure(d, p)
        for side in range(2):
            src, valid, onward, goes = ways(d)[side]

            @pl.when(valid)
            def _():
                arrival(p, (src // 2) * 2 + 1 - h).wait_recv()
                build(p, src // 2)

    def attend(a, state):
        part = pl.ds(a * chunk, chunk)
        g = g_ref[part, :]
        v = v_ref[part, :]
        red = split(red_ref[part, :])
        score = split(jnp.where(lower, dot(g, v, 1, 1), 0.0))
        flipped = split(jnp.where(rows <= cols, dot(v, g, 1, 1), 0.0))
        affinity = split(jnp.where(rows <= cols, mm(red, enlarged[a], 1, 1), 0.0))
        qg = mm([g], split(state * halves[a]), 1, 0) + mm(score, red, 1, 0)
        qg_ref[part, :] = (ups[a] * qg).astype(BF16)
        kpart[part, :] = mm(flipped, enlarged[a], 1, 0)
        vpart[part, :] = mm(affinity, [g], 1, 0)
        if a + 1 < count:
            state = jnp.exp(ends[a]) * state + mm([v], red, 0, 0) * halves[a]
        return state

    def adjoin():
        carry[...] = jnp.zeros_like(carry)
        for d in reversed(range(1, groups)):
            @pl.when(c + d < groups)
            def _():
                group_copy(d).wait_recv()
                size = carry.shape[0]
                carry[...] = arrived[d - 1, 0:size, :] + arrived[d - 1, size:size + 1, :] * carry[...]
        after = carry[...]
        for a in reversed(range(count)):
            part = pl.ds(a * chunk, chunk)
            later = split(after * halves[a])
            kg = kpart[part, :] + mm([v_ref[part, :]], later, 1, 0)
            kg_ref[part, :] = (ed_ref[part, :] * kg).astype(BF16)
            vg = vpart[part, :] + mm(split(red_ref[part, :]), later, 1, 1)
            vg_ref[part, :] = vg.astype(BF16)
            if a > 0:
                after = mstate[a] + jnp.exp(ends[a]) * after

    def multiply(p):
        weights[p].wait()
        for e in range(experts):
            product = dot(slots[p, e], w_ref[p, e], 1, 1)
            if p > 0:
                product = product + sums[e]
            if p < parts - 1:
                sums[e] = product
            else:
                product = product.astype(BF16)
                for src in range(peers):
                    out_ref[0, src, e] = product[src * MOST:(src + 1) * MOST]

    last = line - 1
    for p in range(parts):
        own[p].wait()
        arrival(p, sibling).wait_recv()
        build(p, z)
    state = s_ref[...].T
    done = 0
    for d in range(1, last):
        ensure(d, parts - 1)
        if done < count:
            state = attend(done, state)
            done += 1
        if d + 1 < last:
            for p in range(parts):
                finish(d, p)
    while done < count:
        state = attend(done, state)
        done += 1
    step()
    if last > 1:
        for p in range(parts):
            finish(last - 1, p)
    step()
    adjoin()
    for p in range(parts):
        if last > 0:
            finish(last, p)
        multiply(p)
        step()

    for p in range(parts):
        to_right, to_left, to_sibling = firsts(p)

        @pl.when(z + 1 < line)
        def _():
            to_right.wait_send()

        @pl.when(z >= 1)
        def _():
            to_left.wait_send()

        to_sibling.wait_send()
    for copy in metas:
        copy.wait_send()
    for d in range(1, line):
        for p in range(parts):
            for side in range(2):
                src, valid, goes, on, across = forwards(d, side, p)

                @pl.when(valid)
                def _():
                    @pl.when(goes)
                    def _():
                        on.wait_send()

                    across.wait_send()
    for d in range(1, groups):
        @pl.when(c >= d)
        def _():
            group_copy(d).wait_send()


def deliver(*refs):
    count = (len(refs) - 1) // 2
    sems = refs[-1]
    copies = [pltpu.make_async_copy(refs[i], refs[count + i], sems.at[i]) for i in range(count)]
    for copy in copies:
        copy.start()
    for copy in copies:
        copy.wait()


def local(
    query_heads, key_heads, value_heads, out_grad, log_decay, start_state, layer_grad, gate_weights, routes, expert_down
):
    groups = lax.axis_size("ctx")
    peers = lax.axis_size("exp")
    length, heads, keys = query_heads.shape
    values = value_heads.shape[2]
    tokens, width = layer_grad.shape
    top = routes.shape[1]
    experts, hidden, _ = expert_down.shape
    chunk = min(128, length)
    count = length // chunk
    line = peers // 2
    parts = 3 if width % 384 == 0 else 1
    dma = pltpu.SemaphoreType.DMA
    hbm = pl.BlockSpec(memory_space=pl.ANY)
    shapes = ((length, keys), (length, keys), (length, values), (1, peers, experts, MOST, hidden))
    vmem = pl.BlockSpec(memory_space=pltpu.VMEM)
    held = pl.pallas_call(
        functools.partial(kernel, groups, peers, chunk, parts),
        out_shape=tuple(pltpu.VMEM(shape, BF16) for shape in shapes),
        in_specs=[hbm] * 10,
        out_specs=(vmem,) * 4,
        scratch_shapes=[
            pltpu.VMEM((length, keys), BF16),
            pltpu.VMEM((length, keys), BF16),
            pltpu.VMEM((length, values), BF16),
            pltpu.VMEM((length, values), BF16),
            pltpu.VMEM((length, keys), BF16),
            pltpu.VMEM((keys, values), F32),
            pltpu.VMEM((top, tokens), F32),
            pltpu.VMEM((top, tokens), jnp.int32),
            pltpu.VMEM((peers, 2 * top, tokens), F32),
            pltpu.VMEM((parts, peers * tokens, width // parts), BF16),
            pltpu.VMEM((parts, experts, hidden, width // parts), BF16),
            pltpu.VMEM((line, 2 * experts * MOST, 2 * tokens), BF16),
            pltpu.VMEM((line, 2 * experts * MOST, 128), F32),
            pltpu.VMEM((parts, experts, peers * MOST, width // parts), BF16),
            pltpu.VMEM((experts, peers * MOST, hidden), F32),
            pltpu.VMEM((values + 8, keys), F32),
            pltpu.VMEM((max(1, groups - 1), values + 8, keys), F32),
            pltpu.VMEM((values, keys), F32),
            pltpu.VMEM((length, keys), F32),
            pltpu.VMEM((length, keys), F32),
            pltpu.VMEM((length, keys), F32),
            pltpu.VMEM((length, values), F32),
            pltpu.VMEM((count, values, keys), F32),
            dma((8,)),
            dma((parts,)),
            dma((peers,)),
            dma((peers,)),
            dma((parts, 3)),
            dma((parts,)),
            dma((max(1, line - 1) * 4, parts)),
            dma((parts, peers)),
            dma((max(1, groups - 1),)),
            dma((max(1, groups - 1),)),
        ],
        compiler_params=pltpu.CompilerParams(
            collective_id=0, has_side_effects=True, vmem_limit_bytes=56 * 1024 * 1024
        ),
        cost_estimate=pl.CostEstimate(
            flops=2 * experts * peers * MOST * width * hidden, bytes_accessed=2 * experts * width * hidden, transcendentals=0
        ),
    )(
        query_heads[:, 0, :],
        key_heads[:, 0, :],
        value_heads[:, 0, :],
        out_grad[:, 0, :],
        log_decay[:, 0, :],
        start_state[0, 0],
        layer_grad,
        gate_weights.T,
        routes.T,
        expert_down,
    )
    qg, kg, vg, out = pl.pallas_call(
        deliver,
        out_shape=tuple(jax.ShapeDtypeStruct(shape, BF16) for shape in shapes),
        in_specs=[vmem] * 4,
        out_specs=(hbm,) * 4,
        scratch_shapes=[dma((4,))],
        compiler_params=pltpu.CompilerParams(vmem_limit_bytes=1024 * 1024),
    )(*held)
    return (
        qg.reshape(length, heads, keys),
        kg.reshape(length, heads, keys),
        vg.reshape(length, heads, values),
        out,
    )


def solution(mesh):
    return jax.shard_map(
        local,
        mesh=mesh,
        in_specs=(
            P("ctx", "exp", None),
            P("ctx", "exp", None),
            P("ctx", "exp", None),
            P("ctx", "exp", None),
            P("ctx", "exp", None),
            P("ctx", "exp", None, None),
            P(("ctx", "exp"), None),
            P(("ctx", "exp"), None),
            P(("ctx", "exp"), None),
            P("exp", None, None),
        ),
        out_specs=(
            P("ctx", "exp", None),
            P("ctx", "exp", None),
            P("ctx", "exp", None),
            P("ctx", None, "exp", None, None),
        ),
        check_vma=False,
    )
```

```python
import functools

import jax
import jax.numpy as jnp
from jax import lax
from jax.experimental import pallas as pl
from jax.experimental.pallas import tpu as pltpu
from jax.sharding import PartitionSpec as P

MOST = 16
F32 = jnp.float32
BF16 = jnp.bfloat16
MESH = pl.DeviceIdType.MESH


def dot(a, b, ca, cb):
    return lax.dot_general(a, b, (((ca,), (cb,)), ((), ())), preferred_element_type=F32)


def split(x):
    high = x.astype(BF16)
    return [high, (x - high.astype(F32)).astype(BF16)]


def mm(a, b, ca, cb):
    total = None
    for i, left in enumerate(a):
        for j, right in enumerate(b):
            if i + j < 2:
                term = dot(left, right, ca, cb)
                total = term if total is None else total + term
    return total


def kernel(
    groups, peers, chunk, parts,
    q_hbm, k_hbm, v_hbm, g_hbm, d_hbm, s_hbm, x_hbm, gate_hbm, route_hbm, w_hbm,
    qg_ref, kg_ref, vg_ref, out_ref,
    q_ref, k_ref, v_ref, g_ref, d_ref, s_ref, gate_ref, route_ref, meta, xall, w_ref,
    pick, scale, slots, sums, message, arrived, carry, ed_ref, red_ref,
    kpart, vpart, mstate, lsem, wsem, msend, mrecv, xown, xlocal, xsend, xrecv, csend, crecv,
):
    c = lax.axis_index("ctx")
    s = lax.axis_index("exp")
    z = s // 2
    h = s % 2
    line = peers // 2
    sibling = z * 2 + 1 - h
    length = q_ref.shape[0]
    count = length // chunk
    experts = w_ref.shape[1]
    tokens = x_hbm.shape[0]
    wide = x_hbm.shape[1] // parts

    barrier = pltpu.get_barrier_semaphore()
    for off in range(1, peers):
        pl.semaphore_signal(barrier, inc=1, device_id={"exp": (s + off) % peers}, device_id_type=MESH)
    for off in range(1, groups):
        pl.semaphore_signal(barrier, inc=1, device_id={"ctx": (c + off) % groups}, device_id_type=MESH)

    loads = [
        pltpu.make_async_copy(src, dst, lsem.at[i])
        for i, (src, dst) in enumerate([
            (gate_hbm, gate_ref), (route_hbm, route_ref), (d_hbm, d_ref), (q_hbm, q_ref), (g_hbm, g_ref),
            (k_hbm, k_ref), (v_hbm, v_ref), (s_hbm, s_ref),
        ])
    ]
    def columns(p):
        return pl.ds(p * wide, wide)

    def block(p, src):
        return xall.at[p, pl.ds(pl.multiple_of(src * tokens, tokens), tokens)]

    own = [pltpu.make_async_copy(x_hbm.at[:, columns(p)], block(p, s), xlocal.at[p]) for p in range(parts)]
    for copy in own:
        copy.start()
    for load in loads:
        load.start()
    weights = [pltpu.make_async_copy(w_hbm.at[:, :, columns(p)], w_ref.at[p], wsem.at[p]) for p in range(parts)]
    loads[0].wait()
    loads[1].wait()
    top = gate_ref.shape[0]
    meta[s, 0:top] = gate_ref[...]
    meta[s, top:2 * top] = route_ref[...].astype(F32)

    pl.semaphore_wait(barrier, peers - 1 + groups - 1)

    def send_x(source, p, slot, sem, to):
        return pltpu.make_async_remote_copy(
            src_ref=source, dst_ref=block(p, slot), send_sem=sem, recv_sem=xrecv.at[p, slot],
            device_id={"exp": to}, device_id_type=MESH,
        )

    def firsts(p):
        mine = block(p, s)
        return (
            send_x(mine, p, s, xown.at[p, 0], (s + 2) % peers),
            send_x(mine, p, s, xown.at[p, 1], (s + peers - 2) % peers),
            send_x(mine, p, s, xown.at[p, 2], sibling),
        )

    for p in range(parts):
        own[p].wait()
        to_right, to_left, to_sibling = firsts(p)

        @pl.when(z + 1 < line)
        def _():
            to_right.start()

        @pl.when(z >= 1)
        def _():
            to_left.start()

        to_sibling.start()

    metas = []
    for off in range(1, peers):
        metas.append(pltpu.make_async_remote_copy(
            src_ref=meta.at[s], dst_ref=meta.at[s], send_sem=msend.at[off], recv_sem=mrecv.at[s],
            device_id={"exp": (s + off) % peers}, device_id_type=MESH,
        ))
        metas[-1].start()
    for weight in weights:
        weight.start()

    def ways(d):
        left = (s + peers - 2 * d) % peers
        right = (s + 2 * d) % peers
        return (
            (left, z >= d, (s + 2) % peers, z + 1 < line),
            (right, z + d < line, (s + peers - 2) % peers, z >= 1),
        )

    def forwards(d, side, p):
        src, valid, onward, goes = ways(d)[side]
        row = (d - 1) * 4 + side * 2
        on = send_x(block(p, src), p, src, xsend.at[row, p], onward)
        across = send_x(block(p, src), p, src, xsend.at[row + 1, p], sibling)
        return src, valid, goes, on, across

    def relay(d, p):
        for side in range(2):
            src, valid, goes, on, across = forwards(d, side, p)

            @pl.when(valid)
            def _():
                across.wait_recv()

                @pl.when(goes)
                def _():
                    on.start()

                across.start()

    pending = [(d, p) for d in range(1, line) for p in range(parts)]

    def step():
        if pending:
            relay(*pending.pop(0))

    def ensure(d, p):
        while pending and pending[0] <= (d, p):
            step()

    for load in loads[2:]:
        load.wait()
    rows = lax.broadcasted_iota(jnp.int32, (chunk, chunk), 0)
    cols = lax.broadcasted_iota(jnp.int32, (chunk, chunk), 1)
    lower = rows >= cols
    ones = jnp.where(lower, 1.0, 0.0).astype(BF16)
    ends, halves, ups, enlarged = [], [], [], []
    for a in range(count):
        part = pl.ds(a * chunk, chunk)
        cum = dot(ones, d_ref[part, :], 1, 0)
        end = cum[chunk - 1:chunk, :]
        up = jnp.exp(cum - 0.5 * end)
        ends.append(end)
        halves.append(jnp.exp(0.5 * end))
        ups.append(up)
        enl = split(q_ref[part, :].astype(F32) * up)
        enlarged.append(enl)
        mstate[a] = mm([g_ref[part, :]], enl, 0, 0) * halves[a]
        down = jnp.exp(0.5 * end - cum)
        ed_ref[part, :] = down
        red_ref[part, :] = k_ref[part, :].astype(F32) * down
    total = mstate[count - 1]
    for a in reversed(range(count - 1)):
        total = mstate[a] + jnp.exp(ends[a]) * total
    whole = ends[0]
    for a in range(1, count):
        whole = whole + ends[a]
    keys = message.shape[1]
    message[0:message.shape[0] - 8, :] = total
    message[message.shape[0] - 8:, :] = jnp.broadcast_to(jnp.exp(whole), (8, keys))

    def group_copy(d):
        return pltpu.make_async_remote_copy(
            src_ref=message, dst_ref=arrived.at[d - 1], send_sem=csend.at[d - 1], recv_sem=crecv.at[d - 1],
            device_id={"ctx": (c + groups - d) % groups}, device_id_type=MESH,
        )

    for d in range(1, groups):
        @pl.when(c >= d)
        def _():
            group_copy(d).start()

    before = jnp.where(
        lax.broadcasted_iota(jnp.int32, (tokens, tokens), 0) < lax.broadcasted_iota(jnp.int32, (tokens, tokens), 1), 1.0, 0.0
    ).astype(BF16)
    for off in range(1, peers):
        src = (s + off) % peers
        pltpu.make_async_remote_copy(
            src_ref=meta.at[src], dst_ref=meta.at[src], send_sem=msend.at[0], recv_sem=mrecv.at[src],
            device_id={"exp": sibling}, device_id_type=MESH,
        ).wait_recv()
    gates = meta[:, 0:top]
    routes = meta[:, top:2 * top]
    first = (s * experts).astype(F32)
    place = lax.broadcasted_iota(jnp.int32, (peers, MOST, tokens), 1).astype(F32)
    pair = 2 * MOST
    core = lax.broadcasted_iota(jnp.int32, (line, pair, 2 * tokens), 1) // MOST
    mine = core == lax.broadcasted_iota(jnp.int32, (line, pair, 2 * tokens), 2) // tokens
    for e in range(experts):
        hit = routes == first + e
        member = jnp.sum(jnp.where(hit, 1.0, 0.0), axis=1)
        gate = jnp.sum(jnp.where(hit, gates, 0.0), axis=1)
        earlier = jnp.where(member > 0.5, dot(member.astype(BF16), before, 1, 0), -1.0)
        chosen = jnp.where(earlier[:, None, :] == place, 1.0, 0.0)
        weight = jnp.sum(chosen * gate[:, None, :], axis=2, keepdims=True).reshape(line, pair, 1)
        chosen = chosen.reshape(line, pair, tokens)
        chosen = jnp.where(mine, jnp.concatenate([chosen, chosen], axis=2), 0.0)
        pick[:, e * pair:(e + 1) * pair, :] = chosen.astype(BF16)
        scale[:, e * pair:(e + 1) * pair, :] = jnp.broadcast_to(weight, (line, pair, scale.shape[2]))

    def build(p, chip):
        picked = dot(pick[chip], xall[p, pl.ds(pl.multiple_of(chip * 2 * tokens, 2 * tokens), 2 * tokens), :], 1, 0)
        scaled = (picked * scale[chip][:, 0:1]).astype(BF16)
        for e in range(experts):
            slots[p, e, pl.ds(pl.multiple_of(chip * pair, pair), pair), :] = scaled[e * pair:(e + 1) * pair]

    def arrival(p, src):
        return send_x(block(p, src), p, src, xown.at[p, 2], sibling)

    def finish(d, p):
        ensure(d, p)
        for side in range(2):
            src, valid, onward, goes = ways(d)[side]

            @pl.when(valid)
            def _():
                arrival(p, (src // 2) * 2 + 1 - h).wait_recv()
                build(p, src // 2)

    def attend(a, state):
        part = pl.ds(a * chunk, chunk)
        g = g_ref[part, :]
        v = v_ref[part, :]
        red = split(red_ref[part, :])
        score = split(jnp.where(lower, dot(g, v, 1, 1), 0.0))
        flipped = split(jnp.where(rows <= cols, dot(v, g, 1, 1), 0.0))
        affinity = split(jnp.where(rows <= cols, mm(red, enlarged[a], 1, 1), 0.0))
        qg = mm([g], split(state * halves[a]), 1, 0) + mm(score, red, 1, 0)
        qg_ref[part, :] = (ups[a] * qg).astype(BF16)
        kpart[part, :] = mm(flipped, enlarged[a], 1, 0)
        vpart[part, :] = mm(affinity, [g], 1, 0)
        if a + 1 < count:
            state = jnp.exp(ends[a]) * state + mm([v], red, 0, 0) * halves[a]
        return state

    def adjoin():
        carry[...] = jnp.zeros_like(carry)
        for d in reversed(range(1, groups)):
            @pl.when(c + d < groups)
            def _():
                group_copy(d).wait_recv()
                size = carry.shape[0]
                carry[...] = arrived[d - 1, 0:size, :] + arrived[d - 1, size:size + 1, :] * carry[...]
        after = carry[...]
        for a in reversed(range(count)):
            part = pl.ds(a * chunk, chunk)
            later = split(after * halves[a])
            kg = kpart[part, :] + mm([v_ref[part, :]], later, 1, 0)
            kg_ref[part, :] = (ed_ref[part, :] * kg).astype(BF16)
            vg = vpart[part, :] + mm(split(red_ref[part, :]), later, 1, 1)
            vg_ref[part, :] = vg.astype(BF16)
            if a > 0:
                after = mstate[a] + jnp.exp(ends[a]) * after

    def multiply(p):
        weights[p].wait()
        for e in range(experts):
            product = dot(slots[p, e], w_ref[p, e], 1, 1)
            if p > 0:
                product = product + sums[e]
            if p < parts - 1:
                sums[e] = product
            else:
                product = product.astype(BF16)
                for src in range(peers):
                    out_ref[0, src, e] = product[src * MOST:(src + 1) * MOST]

    last = line - 1
    for p in range(parts):
        arrival(p, sibling).wait_recv()
        build(p, z)
    state = s_ref[...].T
    done = 0
    for d in range(1, last):
        ensure(d, parts - 1)
        if done < count:
            state = attend(done, state)
            done += 1
        if d + 1 < last:
            for p in range(parts):
                finish(d, p)
    while done < count:
        state = attend(done, state)
        done += 1
    if last > 1:
        for p in range(parts):
            finish(last - 1, p)
    step()
    adjoin()
    for p in range(parts):
        if last > 0:
            finish(last, p)
        multiply(p)
        step()

    for p in range(parts):
        to_right, to_left, to_sibling = firsts(p)

        @pl.when(z + 1 < line)
        def _():
            to_right.wait_send()

        @pl.when(z >= 1)
        def _():
            to_left.wait_send()

        to_sibling.wait_send()
    for copy in metas:
        copy.wait_send()
    for d in range(1, line):
        for p in range(parts):
            for side in range(2):
                src, valid, goes, on, across = forwards(d, side, p)

                @pl.when(valid)
                def _():
                    @pl.when(goes)
                    def _():
                        on.wait_send()

                    across.wait_send()
    for d in range(1, groups):
        @pl.when(c >= d)
        def _():
            group_copy(d).wait_send()


def deliver(*refs):
    count = (len(refs) - 1) // 2
    sems = refs[-1]
    copies = [pltpu.make_async_copy(refs[i], refs[count + i], sems.at[i]) for i in range(count)]
    for copy in copies:
        copy.start()
    for copy in copies:
        copy.wait()


def local(
    query_heads, key_heads, value_heads, out_grad, log_decay, start_state, layer_grad, gate_weights, routes, expert_down
):
    groups = lax.axis_size("ctx")
    peers = lax.axis_size("exp")
    length, heads, keys = query_heads.shape
    values = value_heads.shape[2]
    tokens, width = layer_grad.shape
    top = routes.shape[1]
    experts, hidden, _ = expert_down.shape
    chunk = min(128, length)
    count = length // chunk
    line = peers // 2
    parts = 1
    dma = pltpu.SemaphoreType.DMA
    hbm = pl.BlockSpec(memory_space=pl.ANY)
    shapes = ((length, keys), (length, keys), (length, values), (1, peers, experts, MOST, hidden))
    vmem = pl.BlockSpec(memory_space=pltpu.VMEM)
    held = pl.pallas_call(
        functools.partial(kernel, groups, peers, chunk, parts),
        out_shape=tuple(pltpu.VMEM(shape, BF16) for shape in shapes),
        in_specs=[hbm] * 10,
        out_specs=(vmem,) * 4,
        scratch_shapes=[
            pltpu.VMEM((length, keys), BF16),
            pltpu.VMEM((length, keys), BF16),
            pltpu.VMEM((length, values), BF16),
            pltpu.VMEM((length, values), BF16),
            pltpu.VMEM((length, keys), BF16),
            pltpu.VMEM((keys, values), F32),
            pltpu.VMEM((top, tokens), F32),
            pltpu.VMEM((top, tokens), jnp.int32),
            pltpu.VMEM((peers, 2 * top, tokens), F32),
            pltpu.VMEM((parts, peers * tokens, width // parts), BF16),
            pltpu.VMEM((parts, experts, hidden, width // parts), BF16),
            pltpu.VMEM((line, 2 * experts * MOST, 2 * tokens), BF16),
            pltpu.VMEM((line, 2 * experts * MOST, 128), F32),
            pltpu.VMEM((parts, experts, peers * MOST, width // parts), BF16),
            pltpu.VMEM((experts, peers * MOST, hidden), F32),
            pltpu.VMEM((values + 8, keys), F32),
            pltpu.VMEM((max(1, groups - 1), values + 8, keys), F32),
            pltpu.VMEM((values, keys), F32),
            pltpu.VMEM((length, keys), F32),
            pltpu.VMEM((length, keys), F32),
            pltpu.VMEM((length, keys), F32),
            pltpu.VMEM((length, values), F32),
            pltpu.VMEM((count, values, keys), F32),
            dma((8,)),
            dma((parts,)),
            dma((peers,)),
            dma((peers,)),
            dma((parts, 3)),
            dma((parts,)),
            dma((max(1, line - 1) * 4, parts)),
            dma((parts, peers)),
            dma((max(1, groups - 1),)),
            dma((max(1, groups - 1),)),
        ],
        compiler_params=pltpu.CompilerParams(
            collective_id=0, has_side_effects=True, vmem_limit_bytes=56 * 1024 * 1024
        ),
        cost_estimate=pl.CostEstimate(
            flops=2 * experts * peers * MOST * width * hidden, bytes_accessed=2 * experts * width * hidden, transcendentals=0
        ),
    )(
        query_heads[:, 0, :],
        key_heads[:, 0, :],
        value_heads[:, 0, :],
        out_grad[:, 0, :],
        log_decay[:, 0, :],
        start_state[0, 0],
        layer_grad,
        gate_weights.T,
        routes.T,
        expert_down,
    )
    qg, kg, vg, out = pl.pallas_call(
        deliver,
        out_shape=tuple(jax.ShapeDtypeStruct(shape, BF16) for shape in shapes),
        in_specs=[vmem] * 4,
        out_specs=(hbm,) * 4,
        scratch_shapes=[dma((4,))],
        compiler_params=pltpu.CompilerParams(vmem_limit_bytes=1024 * 1024),
    )(*held)
    return (
        qg.reshape(length, heads, keys),
        kg.reshape(length, heads, keys),
        vg.reshape(length, heads, values),
        out,
    )


def solution(mesh):
    return jax.shard_map(
        local,
        mesh=mesh,
        in_specs=(
            P("ctx", "exp", None),
            P("ctx", "exp", None),
            P("ctx", "exp", None),
            P("ctx", "exp", None),
            P("ctx", "exp", None),
            P("ctx", "exp", None, None),
            P(("ctx", "exp"), None),
            P(("ctx", "exp"), None),
            P(("ctx", "exp"), None),
            P("exp", None, None),
        ),
        out_specs=(
            P("ctx", "exp", None),
            P("ctx", "exp", None),
            P("ctx", "exp", None),
            P("ctx", None, "exp", None, None),
        ),
        check_vma=False,
    )
```

```python
import functools

import jax
import jax.numpy as jnp
from jax import lax
from jax.experimental import pallas as pl
from jax.experimental.pallas import tpu as pltpu
from jax.sharding import PartitionSpec as P

MOST = 16
F32 = jnp.float32
BF16 = jnp.bfloat16
MESH = pl.DeviceIdType.MESH


def dot(a, b, ca, cb):
    return lax.dot_general(a, b, (((ca,), (cb,)), ((), ())), preferred_element_type=F32)


def split(x):
    high = x.astype(BF16)
    return [high, (x - high.astype(F32)).astype(BF16)]


def mm(a, b, ca, cb):
    total = None
    for i, left in enumerate(a):
        for j, right in enumerate(b):
            if i + j < 2:
                term = dot(left, right, ca, cb)
                total = term if total is None else total + term
    return total


def kernel(
    groups, peers, chunk, parts,
    q_hbm, k_hbm, v_hbm, g_hbm, d_hbm, s_hbm, x_hbm, gate_hbm, route_hbm, w_hbm,
    qg_ref, kg_ref, vg_ref, out_ref,
    q_ref, k_ref, v_ref, g_ref, d_ref, s_ref, gate_ref, route_ref, meta, xall, w_ref,
    pick, scale, slots, sums, message, arrived, carry, ed_ref, red_ref,
    kpart, vpart, mstate, lsem, wsem, msend, mrecv, xown, xlocal, xsend, xrecv, csend, crecv,
):
    c = lax.axis_index("ctx")
    s = lax.axis_index("exp")
    z = s // 2
    h = s % 2
    line = peers // 2
    sibling = z * 2 + 1 - h
    length = q_ref.shape[0]
    count = length // chunk
    experts = w_ref.shape[1]
    tokens = x_hbm.shape[0]
    wide = x_hbm.shape[1] // parts

    barrier = pltpu.get_barrier_semaphore()
    for off in range(1, peers):
        pl.semaphore_signal(barrier, inc=1, device_id={"exp": (s + off) % peers}, device_id_type=MESH)
    for off in range(1, groups):
        pl.semaphore_signal(barrier, inc=1, device_id={"ctx": (c + off) % groups}, device_id_type=MESH)

    loads = [
        pltpu.make_async_copy(src, dst, lsem.at[i])
        for i, (src, dst) in enumerate([
            (gate_hbm, gate_ref), (route_hbm, route_ref), (d_hbm, d_ref), (q_hbm, q_ref), (g_hbm, g_ref),
            (k_hbm, k_ref), (v_hbm, v_ref), (s_hbm, s_ref),
        ])
    ]
    for load in loads:
        load.start()
    def columns(p):
        return pl.ds(p * wide, wide)

    def block(p, src):
        return xall.at[p, pl.ds(pl.multiple_of(src * tokens, tokens), tokens)]

    own = [pltpu.make_async_copy(x_hbm.at[:, columns(p)], block(p, s), xlocal.at[p]) for p in range(parts)]
    for copy in own:
        copy.start()
    weights = [pltpu.make_async_copy(w_hbm.at[:, :, columns(p)], w_ref.at[p], wsem.at[p]) for p in range(parts)]
    loads[0].wait()
    loads[1].wait()
    top = gate_ref.shape[0]
    meta[s, 0:top] = gate_ref[...]
    meta[s, top:2 * top] = route_ref[...].astype(F32)

    pl.semaphore_wait(barrier, peers - 1 + groups - 1)

    def send_x(source, p, slot, sem, to):
        return pltpu.make_async_remote_copy(
            src_ref=source, dst_ref=block(p, slot), send_sem=sem, recv_sem=xrecv.at[p, slot],
            device_id={"exp": to}, device_id_type=MESH,
        )

    def firsts(p):
        mine = x_hbm.at[:, columns(p)]
        return (
            send_x(mine, p, s, xown.at[p, 0], (s + 2) % peers),
            send_x(mine, p, s, xown.at[p, 1], (s + peers - 2) % peers),
            send_x(mine, p, s, xown.at[p, 2], sibling),
        )

    for p in range(parts):
        to_right, to_left, to_sibling = firsts(p)

        @pl.when(z + 1 < line)
        def _():
            to_right.start()

        @pl.when(z >= 1)
        def _():
            to_left.start()

        to_sibling.start()

    metas = []
    for off in range(1, peers):
        metas.append(pltpu.make_async_remote_copy(
            src_ref=meta.at[s], dst_ref=meta.at[s], send_sem=msend.at[off], recv_sem=mrecv.at[s],
            device_id={"exp": (s + off) % peers}, device_id_type=MESH,
        ))
        metas[-1].start()
    for weight in weights:
        weight.start()

    def ways(d):
        left = (s + peers - 2 * d) % peers
        right = (s + 2 * d) % peers
        return (
            (left, z >= d, (s + 2) % peers, z + 1 < line),
            (right, z + d < line, (s + peers - 2) % peers, z >= 1),
        )

    def forwards(d, side, p):
        src, valid, onward, goes = ways(d)[side]
        row = (d - 1) * 4 + side * 2
        on = send_x(block(p, src), p, src, xsend.at[row, p], onward)
        across = send_x(block(p, src), p, src, xsend.at[row + 1, p], sibling)
        return src, valid, goes, on, across

    def relay(d, p):
        for side in range(2):
            src, valid, goes, on, across = forwards(d, side, p)

            @pl.when(valid)
            def _():
                across.wait_recv()

                @pl.when(goes)
                def _():
                    on.start()

                across.start()

    pending = [(d, p) for d in range(1, line) for p in range(parts)]

    def step():
        if pending:
            relay(*pending.pop(0))

    def ensure(d, p):
        while pending and pending[0] <= (d, p):
            step()

    for load in loads[2:]:
        load.wait()
    rows = lax.broadcasted_iota(jnp.int32, (chunk, chunk), 0)
    cols = lax.broadcasted_iota(jnp.int32, (chunk, chunk), 1)
    lower = rows >= cols
    ones = jnp.where(lower, 1.0, 0.0).astype(BF16)
    ends, halves, ups, enlarged = [], [], [], []
    for a in range(count):
        part = pl.ds(a * chunk, chunk)
        cum = dot(ones, d_ref[part, :], 1, 0)
        end = cum[chunk - 1:chunk, :]
        up = jnp.exp(cum - 0.5 * end)
        ends.append(end)
        halves.append(jnp.exp(0.5 * end))
        ups.append(up)
        enl = split(q_ref[part, :].astype(F32) * up)
        enlarged.append(enl)
        mstate[a] = mm([g_ref[part, :]], enl, 0, 0) * halves[a]
        down = jnp.exp(0.5 * end - cum)
        ed_ref[part, :] = down
        red_ref[part, :] = k_ref[part, :].astype(F32) * down
    total = mstate[count - 1]
    for a in reversed(range(count - 1)):
        total = mstate[a] + jnp.exp(ends[a]) * total
    whole = ends[0]
    for a in range(1, count):
        whole = whole + ends[a]
    keys = message.shape[1]
    message[0:message.shape[0] - 8, :] = total
    message[message.shape[0] - 8:, :] = jnp.broadcast_to(jnp.exp(whole), (8, keys))

    def group_copy(d):
        return pltpu.make_async_remote_copy(
            src_ref=message, dst_ref=arrived.at[d - 1], send_sem=csend.at[d - 1], recv_sem=crecv.at[d - 1],
            device_id={"ctx": (c + groups - d) % groups}, device_id_type=MESH,
        )

    for d in range(1, groups):
        @pl.when(c >= d)
        def _():
            group_copy(d).start()

    before = jnp.where(
        lax.broadcasted_iota(jnp.int32, (tokens, tokens), 0) < lax.broadcasted_iota(jnp.int32, (tokens, tokens), 1), 1.0, 0.0
    ).astype(BF16)
    for off in range(1, peers):
        src = (s + off) % peers
        pltpu.make_async_remote_copy(
            src_ref=meta.at[src], dst_ref=meta.at[src], send_sem=msend.at[0], recv_sem=mrecv.at[src],
            device_id={"exp": sibling}, device_id_type=MESH,
        ).wait_recv()
    gates = meta[:, 0:top]
    routes = meta[:, top:2 * top]
    first = (s * experts).astype(F32)
    place = lax.broadcasted_iota(jnp.int32, (peers, MOST, tokens), 1).astype(F32)
    pair = 2 * MOST
    core = lax.broadcasted_iota(jnp.int32, (line, pair, 2 * tokens), 1) // MOST
    mine = core == lax.broadcasted_iota(jnp.int32, (line, pair, 2 * tokens), 2) // tokens
    for e in range(experts):
        hit = routes == first + e
        member = jnp.sum(jnp.where(hit, 1.0, 0.0), axis=1)
        gate = jnp.sum(jnp.where(hit, gates, 0.0), axis=1)
        earlier = jnp.where(member > 0.5, dot(member.astype(BF16), before, 1, 0), -1.0)
        chosen = jnp.where(earlier[:, None, :] == place, 1.0, 0.0)
        weight = jnp.sum(chosen * gate[:, None, :], axis=2, keepdims=True).reshape(line, pair, 1)
        chosen = chosen.reshape(line, pair, tokens)
        chosen = jnp.where(mine, jnp.concatenate([chosen, chosen], axis=2), 0.0)
        pick[:, e * pair:(e + 1) * pair, :] = chosen.astype(BF16)
        scale[:, e * pair:(e + 1) * pair, :] = jnp.broadcast_to(weight, (line, pair, scale.shape[2]))

    def build(p, chip):
        picked = dot(pick[chip], xall[p, pl.ds(pl.multiple_of(chip * 2 * tokens, 2 * tokens), 2 * tokens), :], 1, 0)
        scaled = (picked * scale[chip][:, 0:1]).astype(BF16)
        for e in range(experts):
            slots[p, e, pl.ds(pl.multiple_of(chip * pair, pair), pair), :] = scaled[e * pair:(e + 1) * pair]

    def arrival(p, src):
        return send_x(block(p, src), p, src, xown.at[p, 2], sibling)

    def finish(d, p):
        ensure(d, p)
        for side in range(2):
            src, valid, onward, goes = ways(d)[side]

            @pl.when(valid)
            def _():
                arrival(p, (src // 2) * 2 + 1 - h).wait_recv()
                build(p, src // 2)

    def attend(a, state):
        part = pl.ds(a * chunk, chunk)
        g = g_ref[part, :]
        v = v_ref[part, :]
        red = split(red_ref[part, :])
        score = split(jnp.where(lower, dot(g, v, 1, 1), 0.0))
        flipped = split(jnp.where(rows <= cols, dot(v, g, 1, 1), 0.0))
        affinity = split(jnp.where(rows <= cols, mm(red, enlarged[a], 1, 1), 0.0))
        qg = mm([g], split(state * halves[a]), 1, 0) + mm(score, red, 1, 0)
        qg_ref[part, :] = (ups[a] * qg).astype(BF16)
        kpart[part, :] = mm(flipped, enlarged[a], 1, 0)
        vpart[part, :] = mm(affinity, [g], 1, 0)
        if a + 1 < count:
            state = jnp.exp(ends[a]) * state + mm([v], red, 0, 0) * halves[a]
        return state

    def adjoin():
        carry[...] = jnp.zeros_like(carry)
        for d in reversed(range(1, groups)):
            @pl.when(c + d < groups)
            def _():
                group_copy(d).wait_recv()
                size = carry.shape[0]
                carry[...] = arrived[d - 1, 0:size, :] + arrived[d - 1, size:size + 1, :] * carry[...]
        after = carry[...]
        for a in reversed(range(count)):
            part = pl.ds(a * chunk, chunk)
            later = split(after * halves[a])
            kg = kpart[part, :] + mm([v_ref[part, :]], later, 1, 0)
            kg_ref[part, :] = (ed_ref[part, :] * kg).astype(BF16)
            vg = vpart[part, :] + mm(split(red_ref[part, :]), later, 1, 1)
            vg_ref[part, :] = vg.astype(BF16)
            if a > 0:
                after = mstate[a] + jnp.exp(ends[a]) * after

    def multiply(p):
        weights[p].wait()
        for e in range(experts):
            product = dot(slots[p, e], w_ref[p, e], 1, 1)
            if p > 0:
                product = product + sums[e]
            if p < parts - 1:
                sums[e] = product
            else:
                product = product.astype(BF16)
                for src in range(peers):
                    out_ref[0, src, e] = product[src * MOST:(src + 1) * MOST]

    last = line - 1
    for p in range(parts):
        own[p].wait()
        arrival(p, sibling).wait_recv()
        build(p, z)
    state = s_ref[...].T
    done = 0
    if last > 0:
        ensure(1, parts - 1)
    state = attend(0, state)
    done = 1
    for d in range(2, last):
        ensure(d, parts - 2)
        for p in range(parts - 1):
            finish(d - 1, p)
        ensure(d, parts - 1)
        if done < count:
            state = attend(done, state)
            done += 1
        finish(d - 1, parts - 1)
    while done < count:
        state = attend(done, state)
        done += 1
    step()
    if last > 1:
        for p in range(parts):
            finish(last - 1, p)
            if p > 0:
                step()
    adjoin()
    for p in range(parts):
        if last > 0:
            finish(last, p)
        multiply(p)

    for p in range(parts):
        to_right, to_left, to_sibling = firsts(p)

        @pl.when(z + 1 < line)
        def _():
            to_right.wait_send()

        @pl.when(z >= 1)
        def _():
            to_left.wait_send()

        to_sibling.wait_send()
    for copy in metas:
        copy.wait_send()
    for d in range(1, line):
        for p in range(parts):
            for side in range(2):
                src, valid, goes, on, across = forwards(d, side, p)

                @pl.when(valid)
                def _():
                    @pl.when(goes)
                    def _():
                        on.wait_send()

                    across.wait_send()
    for d in range(1, groups):
        @pl.when(c >= d)
        def _():
            group_copy(d).wait_send()


def deliver(*refs):
    count = (len(refs) - 1) // 2
    sems = refs[-1]
    copies = [pltpu.make_async_copy(refs[i], refs[count + i], sems.at[i]) for i in range(count)]
    for copy in copies:
        copy.start()
    for copy in copies:
        copy.wait()


def local(
    query_heads, key_heads, value_heads, out_grad, log_decay, start_state, layer_grad, gate_weights, routes, expert_down
):
    groups = lax.axis_size("ctx")
    peers = lax.axis_size("exp")
    length, heads, keys = query_heads.shape
    values = value_heads.shape[2]
    tokens, width = layer_grad.shape
    top = routes.shape[1]
    experts, hidden, _ = expert_down.shape
    chunk = min(128, length)
    count = length // chunk
    line = peers // 2
    parts = 3 if width % 384 == 0 else 1
    dma = pltpu.SemaphoreType.DMA
    hbm = pl.BlockSpec(memory_space=pl.ANY)
    shapes = ((length, keys), (length, keys), (length, values), (1, peers, experts, MOST, hidden))
    vmem = pl.BlockSpec(memory_space=pltpu.VMEM)
    held = pl.pallas_call(
        functools.partial(kernel, groups, peers, chunk, parts),
        out_shape=tuple(pltpu.VMEM(shape, BF16) for shape in shapes),
        in_specs=[hbm] * 10,
        out_specs=(vmem,) * 4,
        scratch_shapes=[
            pltpu.VMEM((length, keys), BF16),
            pltpu.VMEM((length, keys), BF16),
            pltpu.VMEM((length, values), BF16),
            pltpu.VMEM((length, values), BF16),
            pltpu.VMEM((length, keys), BF16),
            pltpu.VMEM((keys, values), F32),
            pltpu.VMEM((top, tokens), F32),
            pltpu.VMEM((top, tokens), jnp.int32),
            pltpu.VMEM((peers, 2 * top, tokens), F32),
            pltpu.VMEM((parts, peers * tokens, width // parts), BF16),
            pltpu.VMEM((parts, experts, hidden, width // parts), BF16),
            pltpu.VMEM((line, 2 * experts * MOST, 2 * tokens), BF16),
            pltpu.VMEM((line, 2 * experts * MOST, 128), F32),
            pltpu.VMEM((parts, experts, peers * MOST, width // parts), BF16),
            pltpu.VMEM((experts, peers * MOST, hidden), F32),
            pltpu.VMEM((values + 8, keys), F32),
            pltpu.VMEM((max(1, groups - 1), values + 8, keys), F32),
            pltpu.VMEM((values, keys), F32),
            pltpu.VMEM((length, keys), F32),
            pltpu.VMEM((length, keys), F32),
            pltpu.VMEM((length, keys), F32),
            pltpu.VMEM((length, values), F32),
            pltpu.VMEM((count, values, keys), F32),
            dma((8,)),
            dma((parts,)),
            dma((peers,)),
            dma((peers,)),
            dma((parts, 3)),
            dma((parts,)),
            dma((max(1, line - 1) * 4, parts)),
            dma((parts, peers)),
            dma((max(1, groups - 1),)),
            dma((max(1, groups - 1),)),
        ],
        compiler_params=pltpu.CompilerParams(
            collective_id=0, has_side_effects=True, vmem_limit_bytes=56 * 1024 * 1024
        ),
        cost_estimate=pl.CostEstimate(
            flops=2 * experts * peers * MOST * width * hidden, bytes_accessed=2 * experts * width * hidden, transcendentals=0
        ),
    )(
        query_heads[:, 0, :],
        key_heads[:, 0, :],
        value_heads[:, 0, :],
        out_grad[:, 0, :],
        log_decay[:, 0, :],
        start_state[0, 0],
        layer_grad,
        gate_weights.T,
        routes.T,
        expert_down,
    )
    qg, kg, vg, out = pl.pallas_call(
        deliver,
        out_shape=tuple(jax.ShapeDtypeStruct(shape, BF16) for shape in shapes),
        in_specs=[vmem] * 4,
        out_specs=(hbm,) * 4,
        scratch_shapes=[dma((4,))],
        compiler_params=pltpu.CompilerParams(vmem_limit_bytes=1024 * 1024),
    )(*held)
    return (
        qg.reshape(length, heads, keys),
        kg.reshape(length, heads, keys),
        vg.reshape(length, heads, values),
        out,
    )


def solution(mesh):
    return jax.shard_map(
        local,
        mesh=mesh,
        in_specs=(
            P("ctx", "exp", None),
            P("ctx", "exp", None),
            P("ctx", "exp", None),
            P("ctx", "exp", None),
            P("ctx", "exp", None),
            P("ctx", "exp", None, None),
            P(("ctx", "exp"), None),
            P(("ctx", "exp"), None),
            P(("ctx", "exp"), None),
            P("exp", None, None),
        ),
        out_specs=(
            P("ctx", "exp", None),
            P("ctx", "exp", None),
            P("ctx", "exp", None),
            P("ctx", None, "exp", None, None),
        ),
        check_vma=False,
    )
```
